32 devices in a mesh: gx: 2 (over core), gy: 4 (over y, x), gz: 4 (over z).
Axes of the slice: x: 2, y: 2, z: 4, core: 2. Of those that a mesh axis runs over, the one named last changes fastest.
Arguments:
- right_side: float32 [32, 256, 512], P('gx', 'gy', 'gz'), may hold values from -18 to 18
- inv_density: float32 [32, 256, 512], P('gx', 'gy', 'gz'), may hold values from 0.5 to 2
- active: int32 [32, 256, 512], P('gx', 'gy', 'gz'), may hold values 0 or 1
Outputs:
- solution_field: float32 [32, 256, 512], P('gx', 'gy', 'gz')
- residual: float32 [32, 256, 512], P('gx', 'gy', 'gz')
The draws below stay inside these ranges and needn't reach their ends.
All inputs are finite; a program needn't handle non-finite values. No bound on the sum of `active` on one device may be relied on, other than what follows from the above.
Results may differ from the reference program's by a relative error of at most 0.0003.
Values sent between devices are 32-bit elements; how exact they have to be, the bound alone decides.
No kernel may reach another device: no remote copies, remote signals or barrier semaphores. Data moves between devices by JAX's collectives and lax.ppermute only.
A program may use at most 64 MiB of HBM per device.

```python
import math
import jax
import jax.numpy as jnp
from jax import lax

STEPS = 6
NX = 32
NY = 256
NZ = 512


def draw_right_side(key, part):
    x_position = lax.broadcasted_iota(jnp.float32, (NX, NY, NZ), 0)
    fraction = x_position / (NX - 1.0)
    rough_part = jnp.clip(jax.random.normal(key, (NX, NY, NZ), jnp.float32), -6.0, 6.0)
    return rough_part * (1.0 + 2.0 * fraction)


def set_ends(entries, stream_key, least, high):
    longest = entries.shape.index(max(entries.shape))
    spots = []
    for shift in (0, 1):
        where = [jax.random.randint(jax.random.fold_in(stream_key, axis), (), 0, length) for axis, length in enumerate(entries.shape)]
        where[longest] = (where[longest] + shift) % entries.shape[longest]
        spots.append(tuple(where))
    return entries.at[spots[0]].set(least).at[spots[1]].set(high)


def block_levels(stream_key, dims, cuts, least, top_value):
    loudness, own = 1.0, jax.random.fold_in(stream_key, 6)
    for position, shards_of in cuts:
        heights = jnp.exp(jax.random.uniform(jax.random.fold_in(own, position), (shards_of,), jnp.float32, least / len(cuts), top_value / len(cuts)))
        loudness = loudness * jnp.repeat(heights, dims[position] // shards_of).reshape([-1 if axis == position else 1 for axis in range(len(dims))])
    return loudness


def setup_inputs(seed: int = 0) -> dict:
    key_list = jax.random.split(jax.random.key(seed), 4)
    right_side = draw_right_side(jax.random.fold_in(key_list[3], 71), 0)
    inv_density = jnp.clip(jnp.exp(math.log(2.0) - 1.3862944 * jax.random.uniform(key_list[1], (NX, NY, NZ), jnp.float32) ** block_levels(key_list[1], (NX, NY, NZ), ((0, 2), (1, 4), (2, 4)), -0.2, 0.2)), 0.5, 2.0)
    active = set_ends((jax.random.randint(key_list[2], (NX, NY, NZ), 0, 4) < 3).astype(jnp.int32), jax.random.fold_in(key_list[2], 1), 0, 1)
    return {"right_side": right_side, "inv_density": inv_density, "active": active}


basis_shift = 7.0
basis_scale = 7.0
NEIGHBOURS = ((2, 1, 1), (0, 1, 1), (1, 2, 1), (1, 0, 1), (1, 1, 2), (1, 1, 0))

def shifted(field, offset):
    extent = field.shape
    return field[offset[0]:extent[0] - 2 + offset[0], offset[1]:extent[1] - 2 + offset[1], offset[2]:extent[2] - 2 + offset[2]]

def apply_valid(vector_pad, weight_pad):
    center_weight = shifted(weight_pad, (1, 1, 1))
    center_value = shifted(vector_pad, (1, 1, 1))
    diagonal = jnp.zeros_like(center_value)
    beside = jnp.zeros_like(center_value)
    for offset in NEIGHBOURS:
        other_weight = shifted(weight_pad, offset)
        other_value = shifted(vector_pad, offset)
        liquid_side = other_weight > 0.0
        denominator = jnp.where(liquid_side, center_weight + other_weight, 1.0)
        face_value = jnp.where(liquid_side, 2.0 * center_weight * other_weight / denominator, center_weight)
        diagonal = diagonal + face_value
        beside = beside + face_value * other_value
    return diagonal * center_value - beside

def next_basis(image_field, previous):
    return (image_field - basis_shift * previous) / basis_scale

def least_squares(triangle):
    column_count = triangle.shape[1] - 1
    row_ids = lax.broadcasted_iota(jnp.int32, (column_count + 1, column_count), 0)
    col_ids = lax.broadcasted_iota(jnp.int32, (column_count + 1, column_count), 1)
    change = jnp.where(row_ids == col_ids, basis_shift, 0.0) + jnp.where(row_ids == col_ids + 1, basis_scale, 0.0)
    change = change.astype(triangle.dtype)
    hess = jnp.dot(triangle, change, precision=lax.Precision.HIGHEST)
    target = triangle[:, 0]
    for pivot_index in range(column_count):
        first_value = hess[pivot_index, pivot_index]
        second_value = hess[pivot_index + 1, pivot_index]
        radius = jnp.sqrt(first_value * first_value + second_value * second_value)
        cosine = first_value / radius
        sine_value = second_value / radius
        upper_row = cosine * hess[pivot_index] + sine_value * hess[pivot_index + 1]
        lower_row = cosine * hess[pivot_index + 1] - sine_value * hess[pivot_index]
        hess = hess.at[pivot_index].set(upper_row).at[pivot_index + 1].set(lower_row)
        upper_target = cosine * target[pivot_index] + sine_value * target[pivot_index + 1]
        lower_target = cosine * target[pivot_index + 1] - sine_value * target[pivot_index]
        target = target.at[pivot_index].set(upper_target).at[pivot_index + 1].set(lower_target)
    solved = [None] * column_count
    for row_index in reversed(range(column_count)):
        running = target[row_index]
        for column_index in range(row_index + 1, column_count):
            running = running - hess[row_index, column_index] * solved[column_index]
        solved[row_index] = running / hess[row_index, row_index]
    coefficients = jnp.stack(solved)
    first_unit = jnp.where(lax.broadcasted_iota(jnp.int32, (column_count + 1,), 0) == 0, 1.0, 0.0).astype(triangle.dtype)
    leftover = first_unit - jnp.dot(change, coefficients, precision=lax.Precision.HIGHEST)
    return (coefficients, leftover)

def reference(right_side, inv_density, active):
    liquid = active.astype(jnp.float32)
    weight = inv_density * liquid
    weight_pad = jnp.pad(weight, 1)
    basis_list = [right_side * liquid]
    for power_index in range(STEPS):
        image_field = apply_valid(jnp.pad(basis_list[-1], 1), weight_pad)
        basis_list.append(next_basis(image_field, basis_list[-1]))
    gram_matrix = jnp.zeros((STEPS + 1, STEPS + 1), jnp.float32)
    for row_index in range(STEPS + 1):
        for column_index in range(row_index + 1):
            product = jnp.sum(basis_list[row_index] * basis_list[column_index])
            gram_matrix = gram_matrix.at[row_index, column_index].set(product).at[column_index, row_index].set(product)
    triangle = jnp.linalg.cholesky(gram_matrix).T
    coefficients, leftover = least_squares(triangle)
    solution_field = jnp.zeros_like(right_side)
    for power_index in range(STEPS):
        solution_field = solution_field + coefficients[power_index] * basis_list[power_index]
    residual = jnp.zeros_like(right_side)
    for power_index in range(STEPS + 1):
        residual = residual + leftover[power_index] * basis_list[power_index]
    return (solution_field, residual)
```

```python
import functools

import jax
import jax.numpy as jnp
from jax import lax
from jax.experimental import pallas as pl
from jax.experimental.pallas import tpu as pltpu
from jax.sharding import PartitionSpec as P

STEPS = 6
SHIFT = 7.0
GROUPS = 8
WIDE = 16
TOP = 8
VMEM = pltpu.VMEM
AXES = ("gx", "gy", "gz")


def vmem_spec():
    return pl.BlockSpec(memory_space=VMEM)


def resident(array):
    return pltpu.with_memory_space_constraint(array, VMEM)


def call(body, outs, name, scratch=(), grid=None, out_specs=None, limit=40, flops=0):
    return pl.pallas_call(
        body,
        out_shape=outs,
        grid=grid or (),
        out_specs=out_specs if out_specs is not None else [vmem_spec() for _ in outs],
        scratch_shapes=list(scratch),
        compiler_params=pltpu.CompilerParams(vmem_limit_bytes=limit << 20),
        cost_estimate=pl.CostEstimate(flops=flops, bytes_accessed=1 << 20, transcendentals=0),
        name=name,
    )


def kept(shape):
    return pltpu.VMEM(shape, jnp.float32)


def lanes(shape=(8, 128)):
    return lax.broadcasted_iota(jnp.int32, shape, len(shape) - 1)


class Plan:
    def __init__(self, mesh, nx, ny, nz):
        self.gx, self.gy, self.gz = (mesh.shape[a] for a in AXES)
        self.nx, self.ny, self.nz = nx, ny, nz
        self.sides = min(self.gx - 1, 2)
        self.planes = nx + STEPS * self.sides
        self.deep = self.planes // GROUPS + 1
        self.rows = ny + 16
        self.half = self.rows // 2
        self.tall = self.rows + 16

    def own(self):
        if self.sides == 1:
            return lax.axis_index("gx") * STEPS
        return STEPS if self.sides == 2 else 0

    def halo_starts(self):
        if self.sides == 1:
            return [(1 - lax.axis_index("gx")) * self.nx]
        return [0, STEPS + self.nx] if self.sides == 2 else []

    def span(self, level):
        if self.sides == 1:
            index = lax.axis_index("gx")
            return level * index, self.planes - level * (1 - index)
        cut = level if self.sides == 2 else 0
        return cut, self.planes - cut


def prepare(plan, rs, inv, act, v, w, *faces):
    for i in range(plan.nx):
        liquid = act[i].astype(jnp.float32)
        v[i] = rs[i] * liquid
        w[i] = inv[i] * liquid
    if plan.sides == 1:
        starts = [(1 - lax.axis_index("gx")) * (plan.nx - STEPS)]
    else:
        starts = [plan.nx - STEPS, 0]
    for start, face in zip(starts, faces):
        for i in range(STEPS):
            face[0, i] = v[start + i]
            face[1, i] = w[start + i]


def pack_rows(plan, v, w, *refs):
    halos, (first, second) = refs[: plan.sides], refs[plan.sides :]
    even = lax.axis_index("gy") % 2 == 0
    for field, own in enumerate((v, w)):
        sources = [(own, (i,)) for i in range(plan.nx)]
        sources += [(halo, (field, i)) for halo in halos for i in range(STEPS)]
        for p, (ref, at) in enumerate(sources):
            low = ref[at + (pl.ds(0, STEPS), slice(None))]
            high = ref[at + (pl.ds(plan.ny - STEPS, STEPS), slice(None))]
            first[field, pl.ds(p * STEPS, STEPS), :] = jnp.where(even, high, low)
            second[field, pl.ds(p * STEPS, STEPS), :] = jnp.where(even, low, high)


def pack_lanes(plan, v, w, *refs):
    halos, refs = refs[: plan.sides], refs[plan.sides :]
    from_first, from_second, v_ext, w_ext, first, second, packed = refs
    ny = plan.ny
    even_y = lax.axis_index("gy") % 2 == 0
    even_z = lax.axis_index("gz") % 2 == 0
    blank = jnp.zeros((plan.tall, 128), jnp.float32)
    lane = lanes()
    group = lane // WIDE
    right_half = (lane % WIDE) >= WIDE // 2
    for field, (own, ext) in enumerate(((v, v_ext), (w, w_ext))):
        for p in (0, plan.planes + 1):
            ext[p] = blank
        sources = [(own, (i,), 1 + plan.own() + i) for i in range(plan.nx)]
        for halo, start in zip(halos, plan.halo_starts()):
            sources += [(halo, (field, i), 1 + start + i) for i in range(STEPS)]
        for p, (ref, at, where) in enumerate(sources):
            one = from_first[field, pl.ds(p * STEPS, STEPS), :]
            two = from_second[field, pl.ds(p * STEPS, STEPS), :]
            ext[where, pl.ds(0, 8), :] = jnp.zeros((8, 128), jnp.float32)
            ext[where, pl.ds(TOP + ny, 24), :] = jnp.zeros((24, 128), jnp.float32)
            ext[where, pl.ds(TOP, ny), :] = ref[at]
            ext[where, pl.ds(TOP - STEPS, STEPS), :] = jnp.where(even_y, two, one)
            ext[where, pl.ds(TOP + ny, STEPS), :] = jnp.where(even_y, one, two)
        for i in range(plan.deep):
            for r in range(plan.rows // 8):
                block = jnp.zeros((8, 128), jnp.float32)
                for g in range(GROUPS):
                    p = g * plan.deep + i
                    if p < plan.planes:
                        moved = pltpu.roll(ext[1 + p, pl.ds(8 * r, 8), :], WIDE * g + 8, 1)
                        block = jnp.where(group == g, moved, block)
                packed[i, pl.ds(8 * r, 8), :] = block
            for r in range(plan.half // 8):
                upper = packed[i, pl.ds(8 * r, 8), :]
                lower = packed[i, pl.ds(plan.half + 8 * r, 8), :]
                to_right = jnp.where(right_half, pltpu.roll(lower, 8, 1), upper)
                to_left = jnp.where(right_half, lower, pltpu.roll(upper, 120, 1))
                first[field, i, pl.ds(8 * r, 8), :] = jnp.where(even_z, to_right, to_left)
                second[field, i, pl.ds(8 * r, 8), :] = jnp.where(even_z, to_left, to_right)


def coupling(one, two):
    total = jnp.maximum(one + two, 0.25)
    inverse = pl.reciprocal(total, approx=True)
    inverse = inverse * (2.0 - total * inverse)
    return (2.0 / SHIFT) * one * two * inverse


def missing(weight, others):
    total = jnp.zeros_like(weight)
    for other in others:
        total = total + jnp.where(other > 0.0, 0.0, weight)
    return total


def krylov(plan, v_ext, w_ext, from_first, from_second, basis, moments, *scratch):
    side_v, side_w, side_next, cx, cy, cz, cm, dg, sx, sy, sz, sm, sd = scratch
    planes, deep, half, tall = plan.planes, plan.deep, plan.half, plan.tall
    even_z = lax.axis_index("gz") % 2 == 0
    lane = lanes()
    group = lane // WIDE
    spot = lane % WIDE
    right_half = spot >= WIDE // 2
    first_lane, last_lane = lane == 0, lane == 127
    blank8 = jnp.zeros((8, 128), jnp.float32)

    for field, side in enumerate((side_v, side_w)):
        for i in range(deep):
            for r in range(half // 8):
                one = from_first[field, i, pl.ds(8 * r, 8), :]
                two = from_second[field, i, pl.ds(8 * r, 8), :]
                left = jnp.where(even_z, two, one)
                right = jnp.where(even_z, one, two)
                side[i, pl.ds(8 * r, 8), :] = jnp.where(right_half, pltpu.roll(right, 8, 1), left)
                side[i, pl.ds(half + 8 * r, 8), :] = jnp.where(
                    right_half, right, pltpu.roll(left, 120, 1)
                )
            side[i, pl.ds(plan.rows, 16), :] = jnp.zeros((16, 128), jnp.float32)

    def beside_main(ref, side, p, i, turn, at):
        center = ref[p, at, :]
        edge = pltpu.roll(side[i, at, :], turn, 1)
        after = pltpu.roll(jnp.where(first_lane, edge, center), 127, 1)
        before = pltpu.roll(jnp.where(last_lane, edge, center), 1, 1)
        return center, after, before

    def beside_side(ref, side, i, at):
        center = side[i, at, :]
        ends = center
        for g in range(GROUPS):
            p = g * deep + i
            if p < planes:
                ends = jnp.where(group == g, pltpu.roll(ref[1 + p, at, :], WIDE * g + 8, 1), ends)
        after = pltpu.roll(jnp.where(spot == 8, ends, center), 127, 1)
        before = pltpu.roll(jnp.where(spot == 7, ends, center), 1, 1)
        return center, after, before

    def next_plane(side, i, at):
        if i < deep - 1:
            return side[i + 1, at, :]
        return pltpu.roll(side[0, at, :], 128 - WIDE, 1)

    def last_plane(side, i, at):
        if i > 0:
            return side[i - 1, at, :]
        return pltpu.roll(side[deep - 1, at, :], WIDE, 1)

    def place(p):
        g = p // deep
        return p - g * deep, 120 - WIDE * g + jnp.where(WIDE * g > 120, 128, 0)

    table_rows = plan.rows
    for i in range(deep):
        for r in range(table_rows // 8):
            at = pl.ds(8 * r, 8)
            here, after, before = beside_side(w_ext, side_w, i, at)
            sx[i, at, :] = coupling(here, next_plane(side_w, i, at))
            sy[i, pl.ds(8 * r + 8, 8), :] = coupling(here, side_w[i, pl.ds(8 * r + 1, 8), :])
            sz[i, at, :] = coupling(here, after)
            sm[i, at, :] = coupling(here, before)
        sy[i, pl.ds(0, 8), :] = blank8
    for i in range(deep):
        for r in range(table_rows // 8):
            at = pl.ds(8 * r, 8)
            here, after, before = beside_side(w_ext, side_w, i, at)
            above = side_w[i, pl.ds(8 * r - 1, 8), :] if r else pltpu.roll(here, 1, 0)
            others = (
                next_plane(side_w, i, at),
                last_plane(side_w, i, at),
                side_w[i, pl.ds(8 * r + 1, 8), :],
                above,
                after,
                before,
            )
            faces = sx[i, at, :] + last_plane(sx, i, at)
            faces = faces + sy[i, pl.ds(8 * r + 8, 8), :] + sy[i, pl.ds(8 * r + 7, 8), :]
            faces = faces + sz[i, at, :] + sm[i, at, :]
            sd[i, at, :] = faces + missing(here, others) * (1.0 / SHIFT) - 1.0

    cx[0] = jnp.zeros((tall, 128), jnp.float32)

    def tables(p, _):
        i, turn = place(p)
        for r in range(table_rows // 8):
            at = pl.ds(8 * r, 8)
            here, after, before = beside_main(w_ext, side_w, 1 + p, i, turn, at)
            cx[1 + p, at, :] = coupling(here, w_ext[2 + p, at, :])
            cy[1 + p, pl.ds(8 * r + 8, 8), :] = coupling(here, w_ext[1 + p, pl.ds(8 * r + 1, 8), :])
            cz[1 + p, at, :] = coupling(here, after)
            cm[1 + p, at, :] = coupling(here, before)
        cy[1 + p, pl.ds(0, 8), :] = blank8
        for r in range(table_rows // 8):
            at = pl.ds(8 * r, 8)
            here, after, before = beside_main(w_ext, side_w, 1 + p, i, turn, at)
            above = w_ext[1 + p, pl.ds(8 * r - 1, 8), :] if r else pltpu.roll(here, 1, 0)
            others = (
                w_ext[2 + p, at, :],
                w_ext[p, at, :],
                w_ext[1 + p, pl.ds(8 * r + 1, 8), :],
                above,
                after,
                before,
            )
            faces = cx[1 + p, at, :] + cx[p, at, :]
            faces = faces + cy[1 + p, pl.ds(8 * r + 8, 8), :] + cy[1 + p, pl.ds(8 * r + 7, 8), :]
            faces = faces + cz[1 + p, at, :] + cm[1 + p, at, :]
            dg[1 + p, at, :] = faces + missing(here, others) * (1.0 / SHIFT) - 1.0
        return 0

    lax.fori_loop(0, planes, tables, 0)

    for k in range(STEPS):
        for p in (0, planes + 1):
            basis[k, p] = jnp.zeros((tall, 128), jnp.float32)

    for level in range(1, STEPS + 1):
        source = v_ext if level == 1 else basis.at[level - 2]
        target = basis.at[level - 1]
        side_from, side_to = (side_v, side_next) if level % 2 else (side_next, side_v)
        start = TOP - STEPS + level
        blocks = -(-(plan.ny + 2 * (STEPS - level)) // 8)

        def step(p, _):
            i, turn = place(p)
            for r in range(blocks):
                s = start + 8 * r
                at = pl.ds(s, 8)
                here, after, before = beside_main(source, side_from, 1 + p, i, turn, at)
                total = cx[1 + p, at, :] * source[2 + p, at, :]
                total = total + cx[p, at, :] * source[p, at, :]
                total = total + cy[1 + p, pl.ds(s + 8, 8), :] * source[1 + p, pl.ds(s + 1, 8), :]
                total = total + cy[1 + p, pl.ds(s + 7, 8), :] * source[1 + p, pl.ds(s - 1, 8), :]
                total = total + cz[1 + p, at, :] * after
                total = total + cm[1 + p, at, :] * before
                target[1 + p, at, :] = dg[1 + p, at, :] * here - total
            return 0

        low, high = plan.span(level)
        lax.fori_loop(low, high, step, 0)
        if level == STEPS:
            break
        for i in range(deep):
            for r in range(blocks):
                s = start + 8 * r
                at = pl.ds(s, 8)
                here, after, before = beside_side(source, side_from, i, at)
                total = sx[i, at, :] * next_plane(side_from, i, at)
                total = total + last_plane(sx, i, at) * last_plane(side_from, i, at)
                total = total + sy[i, pl.ds(s + 8, 8), :] * side_from[i, pl.ds(s + 1, 8), :]
                total = total + sy[i, pl.ds(s + 7, 8), :] * side_from[i, pl.ds(s - 1, 8), :]
                total = total + sz[i, at, :] * after
                total = total + sm[i, at, :] * before
                side_to[i, at, :] = sd[i, at, :] * here - total

    own = 1 + plan.own()

    def products(p, sums):
        sums = list(sums)
        for r in range(plan.ny // 8):
            at = pl.ds(TOP + 8 * r, 8)
            fields = [v_ext[own + p, at, :]] + [basis[k, own + p, at, :] for k in range(STEPS)]
            for k in range(STEPS + 1):
                sums[2 * k] = sums[2 * k] + fields[k] * fields[k]
                if k < STEPS:
                    sums[2 * k + 1] = sums[2 * k + 1] + fields[k] * fields[k + 1]
        return tuple(sums)

    sums = lax.fori_loop(0, plan.nx, products, (blank8,) * (2 * STEPS + 1))
    line = jnp.zeros((1, 128), jnp.float32)
    for j, part in enumerate(sums):
        line = jnp.where(lanes((1, 128)) == j, jnp.sum(part), line)
    for j in range(moments.shape[0]):
        moments[j] = line


def weigh(parts):
    line = jnp.sum(parts, axis=0)
    line = jnp.broadcast_to(line, (8, 128))
    moment = []
    for j in range(2 * STEPS + 1):
        picked = jnp.where(lanes() == j, line, 0.0)
        moment.append(jnp.broadcast_to(jnp.sum(picked, axis=1, keepdims=True), (8, 128)))
    count = STEPS + 1
    gram = [[moment[i + j] for j in range(count)] for i in range(count)]
    sign = [1.0 if k % 2 == 0 else -1.0 for k in range(count)]
    rhs = [jnp.full((8, 128), s, jnp.float32) for s in sign]
    inverse = []
    for p in range(count):
        inverse.append(1.0 / gram[p][p])
        for i in range(p + 1, count):
            factor = gram[p][i] * inverse[p]
            for j in range(i, count):
                gram[i][j] = gram[i][j] - factor * gram[p][j]
            rhs[i] = rhs[i] - factor * rhs[p]
    solved = [None] * count
    for p in reversed(range(count)):
        running = rhs[p]
        for j in range(p + 1, count):
            running = running - gram[p][j] * solved[j]
        solved[p] = running * inverse[p]
    scale = sign[0] * solved[0]
    for k in range(1, count):
        scale = scale + sign[k] * solved[k]
    scale = 1.0 / scale
    leftover = [s * scale for s in solved]
    coefficients = [(1.0 - leftover[0]) * (1.0 / SHIFT)]
    for k in range(1, STEPS):
        coefficients.append(leftover[k] * (-1.0 / SHIFT) - coefficients[-1])
    return coefficients, leftover


def combine(plan, chunk, parts, v_ext, basis, solution_field, residual, weights):
    @pl.when(pl.program_id(0) == 0)
    def _():
        coefficients, leftover = weigh(parts[...])
        for k, value in enumerate(coefficients + leftover):
            weights[k] = value

    own = 1 + plan.own() + pl.program_id(0) * chunk

    def plane(p, _):
        for r in range(plan.ny // 8):
            at = pl.ds(TOP + 8 * r, 8)
            fields = [v_ext[own + p, at, :]] + [basis[k, own + p, at, :] for k in range(STEPS)]
            out = weights[0] * fields[0]
            for k in range(1, STEPS):
                out = out + weights[k] * fields[k]
            solution_field[p, pl.ds(8 * r, 8), :] = out
            out = weights[STEPS] * fields[0]
            for k in range(1, STEPS + 1):
                out = out + weights[STEPS + k] * fields[k]
            residual[p, pl.ds(8 * r, 8), :] = out
        return 0

    lax.fori_loop(0, chunk, plane, 0)


def swaps(first, second, axis):
    count = lax.axis_size(axis)
    ones = [(i, i + 1) for i in range(0, count - 1, 2)]
    twos = [(i, i + 1) for i in range(1, count - 1, 2)]
    return tuple(
        lax.ppermute(value, axis, pairs + [(b, a) for a, b in pairs])
        for value, pairs in ((first, ones), (second, twos))
    )


def on_device(mesh, right_side, inv_density, active):
    nx, ny, nz = right_side.shape
    plan = Plan(mesh, nx, ny, nz)
    field = kept((nx, ny, nz))
    face = kept((2, STEPS, ny, nz))
    v, w, *faces = call(
        functools.partial(prepare, plan), [field, field] + [face] * plan.sides, "prepare"
    )(right_side, inv_density, active)
    if plan.sides == 1:
        halos = [lax.ppermute(faces[0], "gx", [(0, 1), (1, 0)])]
    else:
        steps = [(i, i + 1) for i in range(plan.gx - 1)]
        pairs = [steps, [(b, a) for a, b in steps]]
        halos = [lax.ppermute(f, "gx", p) for f, p in zip(faces, pairs)]
    v, w, *halos = [resident(a) for a in [v, w] + halos]
    strip = kept((2, plan.planes * STEPS, 128))
    first, second = call(functools.partial(pack_rows, plan), [strip, strip], "rows")(v, w, *halos)
    first, second = swaps(first, second, "gy")
    extended = kept((plan.planes + 2, plan.tall, 128))
    column = kept((2, plan.deep, plan.half, 128))
    v_ext, w_ext, first, second = call(
        functools.partial(pack_lanes, plan),
        [extended, extended, column, column],
        "columns",
        scratch=[kept((plan.deep, plan.rows, 128))],
    )(v, w, *halos, resident(first), resident(second))
    first, second = swaps(first, second, "gz")
    v_ext = resident(v_ext)
    devices = plan.gx * plan.gy * plan.gz
    side = (plan.deep, plan.tall, 128)
    table = (plan.planes + 2, plan.tall, 128)
    basis, moments = call(
        functools.partial(krylov, plan),
        [kept((STEPS,) + table), kept((devices, 1, 128))],
        "krylov",
        scratch=[kept(side)] * 3 + [kept(table)] * 5 + [kept(side)] * 5,
    )(v_ext, resident(w_ext), resident(first), resident(second))
    parts = lax.all_to_all(moments, AXES, 0, 0, tiled=True)
    chunk = 4
    block = pl.BlockSpec((chunk, ny, nz), lambda i: (i, 0, 0))
    shape = jax.ShapeDtypeStruct((nx, ny, nz), jnp.float32)
    out, residual = pl.pallas_call(
        functools.partial(combine, plan, chunk),
        out_shape=[shape, shape],
        grid=(nx // chunk,),
        in_specs=[vmem_spec()] * 3,
        out_specs=[block, block],
        scratch_shapes=[kept((2 * STEPS + 1, 8, 128))],
        compiler_params=pltpu.CompilerParams(vmem_limit_bytes=40 << 20),
        name="combine",
    )(resident(parts), v_ext, resident(basis))
    return out, residual


def solution(mesh):
    placed = P("gx", "gy", "gz")
    return jax.shard_map(
        functools.partial(on_device, mesh),
        mesh=mesh,
        in_specs=(placed,) * 3,
        out_specs=(placed, placed),
        check_vma=False,
    )
```

```python
import functools

import jax
import jax.numpy as jnp
from jax import lax
from jax.experimental import pallas as pl
from jax.experimental.pallas import tpu as pltpu
from jax.sharding import PartitionSpec as P

STEPS = 6
SHIFT = 7.0
GROUPS = 8
WIDE = 16
RIMS = 3
BAND = 40
UNROLL = 3
TOP = 8
VMEM = pltpu.VMEM
AXES = ("gx", "gy", "gz")


def vmem_spec():
    return pl.BlockSpec(memory_space=VMEM)


def resident(array):
    return pltpu.with_memory_space_constraint(array, VMEM)


def call(body, outs, name, scratch=(), grid=None, out_specs=None, limit=40, flops=0):
    return pl.pallas_call(
        body,
        out_shape=outs,
        grid=grid or (),
        out_specs=out_specs if out_specs is not None else [vmem_spec() for _ in outs],
        scratch_shapes=list(scratch),
        compiler_params=pltpu.CompilerParams(vmem_limit_bytes=limit << 20),
        cost_estimate=pl.CostEstimate(flops=flops, bytes_accessed=1 << 20, transcendentals=0),
        name=name,
    )


def kept(shape):
    return pltpu.VMEM(shape, jnp.float32)


def lanes(shape=(8, 128)):
    return lax.broadcasted_iota(jnp.int32, shape, len(shape) - 1)


class Plan:
    def __init__(self, mesh, nx, ny, nz):
        self.gx, self.gy, self.gz = (mesh.shape[a] for a in AXES)
        self.nx, self.ny, self.nz = nx, ny, nz
        self.sides = min(self.gx - 1, 2)
        self.planes = nx + STEPS * self.sides
        self.deep = self.planes // GROUPS + 1
        self.rows = ny + 16
        self.half = self.rows // 2
        self.tall = self.rows + 16
        self.rim = self.planes // RIMS + 1

    def own(self):
        if self.sides == 1:
            return lax.axis_index("gx") * STEPS
        return STEPS if self.sides == 2 else 0

    def halo_starts(self):
        if self.sides == 1:
            return [(1 - lax.axis_index("gx")) * self.nx]
        return [0, STEPS + self.nx] if self.sides == 2 else []

    def span(self, level):
        if self.sides == 1:
            index = lax.axis_index("gx")
            return level * index, self.planes - level
        cut = level if self.sides == 2 else 0
        return cut, self.planes - 2 * cut


def prepare(plan, rs, inv, act, v, w, *faces):
    for i in range(plan.nx):
        liquid = act[i].astype(jnp.float32)
        v[i] = rs[i] * liquid
        w[i] = inv[i] * liquid * (2.0 / SHIFT)
    if plan.sides == 1:
        starts = [(1 - lax.axis_index("gx")) * (plan.nx - STEPS)]
    else:
        starts = [plan.nx - STEPS, 0]
    for start, face in zip(starts, faces):
        for i in range(STEPS):
            face[0, i] = v[start + i]
            face[1, i] = w[start + i]


def pack_rows(plan, v, w, *refs):
    halos, (first, second) = refs[: plan.sides], refs[plan.sides :]
    even = lax.axis_index("gy") % 2 == 0
    for field, own in enumerate((v, w)):
        sources = [(own, (i,)) for i in range(plan.nx)]
        sources += [(halo, (field, i)) for halo in halos for i in range(STEPS)]
        for p, (ref, at) in enumerate(sources):
            low = ref[at + (pl.ds(0, STEPS), slice(None))]
            high = ref[at + (pl.ds(plan.ny - STEPS, STEPS), slice(None))]
            first[field, pl.ds(p * STEPS, STEPS), :] = jnp.where(even, high, low)
            second[field, pl.ds(p * STEPS, STEPS), :] = jnp.where(even, low, high)


def pack_lanes(plan, v, w, *refs):
    halos, refs = refs[: plan.sides], refs[plan.sides :]
    from_first, from_second, v_ext, w_ext, first, second, packed = refs
    ny = plan.ny
    even_y = lax.axis_index("gy") % 2 == 0
    even_z = lax.axis_index("gz") % 2 == 0
    blank = jnp.zeros((plan.tall, 128), jnp.float32)
    lane = lanes()
    group = lane // WIDE
    right_half = (lane % WIDE) >= WIDE // 2
    for field, (own, ext) in enumerate(((v, v_ext), (w, w_ext))):
        ext[0] = blank
        for p in range(plan.planes + 1, ext.shape[0]):
            ext[p] = blank
        sources = [(own, (i,), 1 + plan.own() + i) for i in range(plan.nx)]
        for halo, start in zip(halos, plan.halo_starts()):
            sources += [(halo, (field, i), 1 + start + i) for i in range(STEPS)]
        for p, (ref, at, where) in enumerate(sources):
            one = from_first[field, pl.ds(p * STEPS, STEPS), :]
            two = from_second[field, pl.ds(p * STEPS, STEPS), :]
            ext[where, pl.ds(0, 8), :] = jnp.zeros((8, 128), jnp.float32)
            ext[where, pl.ds(TOP + ny, 24), :] = jnp.zeros((24, 128), jnp.float32)
            ext[where, pl.ds(TOP, ny), :] = ref[at]
            ext[where, pl.ds(TOP - STEPS, STEPS), :] = jnp.where(even_y, two, one)
            ext[where, pl.ds(TOP + ny, STEPS), :] = jnp.where(even_y, one, two)
        for i in range(plan.deep):
            for r in range(plan.rows // 8):
                block = jnp.zeros((8, 128), jnp.float32)
                for g in range(GROUPS):
                    p = g * plan.deep + i
                    if p < plan.planes:
                        moved = pltpu.roll(ext[1 + p, pl.ds(8 * r, 8), :], WIDE * g + 8, 1)
                        block = jnp.where(group == g, moved, block)
                packed[i, pl.ds(8 * r, 8), :] = block
            for r in range(plan.half // 8):
                upper = packed[i, pl.ds(8 * r, 8), :]
                lower = packed[i, pl.ds(plan.half + 8 * r, 8), :]
                to_right = jnp.where(right_half, pltpu.roll(lower, 8, 1), upper)
                to_left = jnp.where(right_half, lower, pltpu.roll(upper, 120, 1))
                first[field, i, pl.ds(8 * r, 8), :] = jnp.where(even_z, to_right, to_left)
                second[field, i, pl.ds(8 * r, 8), :] = jnp.where(even_z, to_left, to_right)


def coupling(one, two):
    total = jnp.maximum(one + two, 0.0625)
    inverse = pl.reciprocal(total, approx=True)
    inverse = inverse * (2.0 - total * inverse)
    return (one * two) * inverse


def face_tables(weight, tables, planes, blocks):
    cx, cy, cz, dg = tables

    def faces(p, _):
        for r in range(blocks):
            at = pl.ds(8 * r, 8)
            here = weight[p, at, :]
            cx[p, at, :] = coupling(here, weight[p + 1, at, :])
            cy[p, pl.ds(8 * r + 8, 8), :] = coupling(here, weight[p, pl.ds(8 * r + 1, 8), :])
            cz[p, at, :] = coupling(here, pltpu.roll(here, 127, 1))
        return 0

    lax.fori_loop(0, planes + 1, faces, 0)

    def diagonal(trip, _):
        for u in range(2):
            p = 1 + 2 * trip + u
            for r in range(blocks):
                at = pl.ds(8 * r, 8)
                air = 0.5 * weight[p, at, :]
                total = jnp.full((8, 128), -1.0, jnp.float32)
                ahead = cz[p, at, :]
                for face in (
                    cx[p, at, :],
                    cx[p - 1, at, :],
                    cy[p, pl.ds(8 * r + 8, 8), :],
                    cy[p, pl.ds(8 * r + 7, 8), :],
                    ahead,
                    pltpu.roll(ahead, 1, 1),
                ):
                    total = total + jnp.where(face > 0.0, face, air)
                dg[p, at, :] = total
        return 0

    lax.fori_loop(0, (planes + 1) // 2, diagonal, 0)


def advance(source, target, tables, first, trips, unroll, start, blocks):
    cx, cy, cz, dg = tables

    def body(trip, _):
        base = first + trip * unroll
        for r in range(blocks):
            s = start + 8 * r
            at = pl.ds(s, 8)
            fields = [source[base + u, at, :] for u in range(unroll + 2)]
            walls = [cx[base + u, at, :] for u in range(unroll + 1)]
            for u in range(unroll):
                p = base + u + 1
                here, ahead = fields[u + 1], cz[p, at, :]
                after = pltpu.roll(here, 127, 1)
                behind = pltpu.roll(ahead * here, 1, 1)
                total = walls[u + 1] * fields[u + 2] + walls[u] * fields[u]
                total = total + cy[p, pl.ds(s + 8, 8), :] * source[p, pl.ds(s + 1, 8), :]
                total = total + cy[p, pl.ds(s + 7, 8), :] * source[p, pl.ds(s - 1, 8), :]
                total = total + (ahead * after + behind)
                target[p, at, :] = dg[p, at, :] * here - total
        return 0

    lax.fori_loop(0, trips, body, 0)


def level_rows(plan, level):
    return TOP - STEPS + level, -(-(plan.ny + 2 * (STEPS - level)) // 8)


def products(fields, sums):
    for k in range(STEPS + 1):
        sums[2 * k] = sums[2 * k] + fields[k] * fields[k]
        if k < STEPS:
            sums[2 * k + 1] = sums[2 * k + 1] + fields[k] * fields[k + 1]
    return sums


def inner(plan, v_ext, w_ext, *refs):
    basis, (sums_ref, rim_v, rim_w), tables = refs[:STEPS], refs[STEPS : STEPS + 3], refs[STEPS + 3 :]
    planes = plan.planes
    blank8 = jnp.zeros((8, 128), jnp.float32)
    face_tables(w_ext, tables, planes, plan.rows // 8)
    for ref in basis:
        ref[0] = jnp.zeros(ref.shape[1:], jnp.float32)
        ref[planes + 1] = jnp.zeros(ref.shape[1:], jnp.float32)
    source = v_ext
    for level in range(1, STEPS + 1):
        low, count = plan.span(level)
        trips = -(-count // UNROLL)
        low = jnp.minimum(low, planes - UNROLL * trips)
        start, blocks = level_rows(plan, level)
        advance(source, basis[level - 1], tables, low, trips, UNROLL, start, blocks)
        source = basis[level - 1]

    own = 1 + plan.own()

    def gather(p, sums):
        sums = list(sums)
        for r in range(plan.ny // 8):
            at = pl.ds(TOP + 8 * r, 8)
            sums = products([ref[own + p, at, :] for ref in (v_ext,) + tuple(basis)], sums)
        return tuple(sums)

    sums = lax.fori_loop(0, plan.nx, gather, (blank8,) * (2 * STEPS + 1))
    lane = lanes()
    fresh = (lane >= STEPS) & (lane < 128 - STEPS)
    for j, part in enumerate(sums):
        sums_ref[j] = jnp.where(fresh, part, 0.0)

    band, spot = lane // BAND, lane % BAND
    for ext, rim in ((v_ext, rim_v), (w_ext, rim_w)):
        def fill(r, _):
            at = pl.ds(pl.multiple_of(8 * r, 8), 8)
            for i in range(plan.rim):
                block = blank8
                for g in range(RIMS):
                    p = g * plan.rim + i
                    if p < planes:
                        value = ext[1 + p, at, :]
                        high = pltpu.roll(value, BAND * g + 12, 1)
                        low = pltpu.roll(value, (BAND * g + 28) % 128, 1)
                        block = jnp.where((band == g) & (spot < 12), high, block)
                        block = jnp.where((band == g) & (spot >= 28), low, block)
                rim[1 + i, at, :] = block
            return 0

        lax.fori_loop(0, plan.rows // 8, fill, 0)


def outer(plan, first, second, rim_v, rim_w, sums_ref, *refs):
    basis, (moments, rim_0, rim_s), tables = refs[:STEPS], refs[STEPS : STEPS + 3], refs[STEPS + 3 :]
    planes, deep, half, rim = plan.planes, plan.deep, plan.half, plan.rim
    even_z = lax.axis_index("gz") % 2 == 0
    lane = lanes()
    right_half = (lane % WIDE) >= WIDE // 2
    band, spot = lane // BAND, lane % BAND
    halo = (spot >= 12) & (spot < 28)
    blank8 = jnp.zeros((8, 128), jnp.float32)

    def wrap(ref, start, blocks):
        for r in range(blocks):
            at = pl.ds(start + 8 * r, 8)
            ref[0, at, :] = pltpu.roll(ref[rim, at, :], BAND, 1)
            ref[rim + 1, at, :] = pltpu.roll(ref[1, at, :], 128 - BAND, 1)

    for field, (own, full) in enumerate(((rim_v, rim_0), (rim_w, rim_s))):
        columns = [[None] * (2 * (half // 8)) for _ in range(deep)]
        for i in range(deep):
            for r in range(half // 8):
                one = first[field, i, pl.ds(8 * r, 8), :]
                two = second[field, i, pl.ds(8 * r, 8), :]
                left = jnp.where(even_z, two, one)
                right = jnp.where(even_z, one, two)
                columns[i][r] = jnp.where(right_half, pltpu.roll(left, 8, 1), right)
                columns[i][half // 8 + r] = jnp.where(right_half, left, pltpu.roll(right, 120, 1))
        for r in range(plan.rows // 8):
            at = pl.ds(8 * r, 8)
            for i in range(rim):
                block = own[1 + i, at, :]
                for g in range(RIMS):
                    p = g * rim + i
                    if p < planes:
                        turn = (BAND * g + 12 - WIDE * (p // deep)) % 128
                        moved = pltpu.roll(columns[p % deep][r], turn, 1)
                        block = jnp.where((band == g) & halo, moved, block)
                full[1 + i, at, :] = block
        for i in range(rim + 2):
            full[i, pl.ds(plan.rows, 16), :] = jnp.zeros((16, 128), jnp.float32)
        wrap(full, 0, plan.rows // 8)

    face_tables(rim_s, tables, rim, plan.rows // 8)
    source = rim_0
    for level in range(1, STEPS + 1):
        start, blocks = level_rows(plan, level)
        advance(source, basis[level - 1], tables, 0, rim // 2, 2, start, blocks)
        source = basis[level - 1]
        if level < STEPS:
            wrap(source, start, blocks)

    own = plan.own()
    fresh = ((spot >= 6) & (spot < 12)) | ((spot >= 28) & (spot < 34))
    sums = [sums_ref[j] for j in range(2 * STEPS + 1)]
    for i in range(rim):
        part = [blank8] * (2 * STEPS + 1)
        for r in range(plan.ny // 8):
            at = pl.ds(TOP + 8 * r, 8)
            part = products([ref[1 + i, at, :] for ref in (rim_0,) + tuple(basis)], part)
        plane = band * rim + i
        mine = fresh & (plane >= own) & (plane < own + plan.nx)
        sums = [a + jnp.where(mine, b, 0.0) for a, b in zip(sums, part)]
    line = jnp.zeros((1, 128), jnp.float32)
    for j, part in enumerate(sums):
        line = jnp.where(lanes((1, 128)) == j, jnp.sum(part), line)
    for j in range(moments.shape[0]):
        moments[j] = line


def weigh(parts):
    line = jnp.sum(parts, axis=0)
    line = jnp.broadcast_to(line, (8, 128))
    moment = []
    for j in range(2 * STEPS + 1):
        picked = jnp.where(lanes() == j, line, 0.0)
        moment.append(jnp.broadcast_to(jnp.sum(picked, axis=1, keepdims=True), (8, 128)))
    count = STEPS + 1
    gram = [[moment[i + j] for j in range(count)] for i in range(count)]
    sign = [1.0 if k % 2 == 0 else -1.0 for k in range(count)]
    rhs = [jnp.full((8, 128), s, jnp.float32) for s in sign]
    inverse = []
    for p in range(count):
        inverse.append(1.0 / gram[p][p])
        for i in range(p + 1, count):
            factor = gram[p][i] * inverse[p]
            for j in range(i, count):
                gram[i][j] = gram[i][j] - factor * gram[p][j]
            rhs[i] = rhs[i] - factor * rhs[p]
    solved = [None] * count
    for p in reversed(range(count)):
        running = rhs[p]
        for j in range(p + 1, count):
            running = running - gram[p][j] * solved[j]
        solved[p] = running * inverse[p]
    scale = sign[0] * solved[0]
    for k in range(1, count):
        scale = scale + sign[k] * solved[k]
    scale = 1.0 / scale
    leftover = [s * scale for s in solved]
    coefficients = [(1.0 - leftover[0]) * (1.0 / SHIFT)]
    for k in range(1, STEPS):
        coefficients.append(leftover[k] * (-1.0 / SHIFT) - coefficients[-1])
    return coefficients, leftover


def combine(plan, chunk, parts, v_ext, rim_0, *refs):
    basis, rims = refs[:STEPS], refs[STEPS : 2 * STEPS]
    solution_field, residual, weights = refs[2 * STEPS :]

    @pl.when(pl.program_id(0) == 0)
    def _():
        coefficients, leftover = weigh(parts[...])
        for k, value in enumerate(coefficients + leftover):
            weights[k] = value

    own = plan.own() + pl.program_id(0) * chunk
    lane = lanes()

    def mix(refs, p, at):
        fields = [ref[p, at, :] for ref in refs]
        one, two = weights[0] * fields[0], weights[STEPS] * fields[0]
        for k in range(1, STEPS):
            one = one + weights[k] * fields[k]
            two = two + weights[STEPS + k] * fields[k]
        return one, two + weights[2 * STEPS] * fields[STEPS]

    for p in range(chunk):
        plane = own + p
        band = plane // plan.rim
        depth = plane - band * plan.rim
        low = 100 - BAND * band
        low = jnp.where(low < 0, low + 128, low)
        high = 116 - BAND * band
        for r in range(plan.ny // 8):
            at = pl.ds(TOP + 8 * r, 8)
            mains = mix((v_ext,) + tuple(basis), 1 + plane, at)
            edges = mix((rim_0,) + tuple(rims), 1 + depth, at)
            for out, main, edge in zip((solution_field, residual), mains, edges):
                value = jnp.where(lane < STEPS, pltpu.roll(edge, low, 1), main)
                value = jnp.where(lane >= 128 - STEPS, pltpu.roll(edge, high, 1), value)
                out[p, pl.ds(8 * r, 8), :] = value


def swaps(first, second, axis):
    count = lax.axis_size(axis)
    ones = [(i, i + 1) for i in range(0, count - 1, 2)]
    twos = [(i, i + 1) for i in range(1, count - 1, 2)]
    return tuple(
        lax.ppermute(value, axis, pairs + [(b, a) for a, b in pairs])
        for value, pairs in ((first, ones), (second, twos))
    )


def on_device(mesh, right_side, inv_density, active):
    nx, ny, nz = right_side.shape
    plan = Plan(mesh, nx, ny, nz)
    field = kept((nx, ny, nz))
    face = kept((2, STEPS, ny, nz))
    v, w, *faces = call(
        functools.partial(prepare, plan), [field, field] + [face] * plan.sides, "prepare"
    )(right_side, inv_density, active)
    if plan.sides == 1:
        halos = [lax.ppermute(faces[0], "gx", [(0, 1), (1, 0)])]
    else:
        steps = [(i, i + 1) for i in range(plan.gx - 1)]
        pairs = [steps, [(b, a) for a, b in steps]]
        halos = [lax.ppermute(f, "gx", p) for f, p in zip(faces, pairs)]
    v, w, *halos = [resident(a) for a in [v, w] + halos]
    strip = kept((2, plan.planes * STEPS, 128))
    first, second = call(functools.partial(pack_rows, plan), [strip, strip], "rows")(v, w, *halos)
    first, second = swaps(first, second, "gy")
    table = kept((plan.planes + 2, plan.tall, 128))
    column = kept((2, plan.deep, plan.half, 128))
    v_ext, w_ext, first, second = call(
        functools.partial(pack_lanes, plan),
        [table, table, column, column],
        "columns",
        scratch=[kept((plan.deep, plan.rows, 128))],
    )(v, w, *halos, resident(first), resident(second))
    first, second = swaps(first, second, "gz")
    v_ext, w_ext = resident(v_ext), resident(w_ext)
    devices = plan.gx * plan.gy * plan.gz
    rim = kept((plan.rim + 2, plan.tall, 128))
    sums = kept((2 * STEPS + 1, 8, 128))
    *basis, sums, rim_v, rim_w = call(
        functools.partial(inner, plan),
        [table] * STEPS + [sums, rim, rim],
        "inner",
        scratch=[table] * 4,
        flops=1 << 24,
    )(v_ext, w_ext)
    *rims, moments, rim_0 = call(
        functools.partial(outer, plan),
        [rim] * STEPS + [kept((devices, 1, 128)), rim],
        "outer",
        scratch=[rim] * 5,
    )(*[resident(a) for a in (first, second, rim_v, rim_w, sums)])
    parts = lax.all_to_all(moments, AXES, 0, 0, tiled=True)
    chunk = 4
    block = pl.BlockSpec((chunk, ny, nz), lambda i: (i, 0, 0))
    shape = jax.ShapeDtypeStruct((nx, ny, nz), jnp.float32)
    operands = [parts, v_ext, rim_0] + basis + rims
    out, residual = pl.pallas_call(
        functools.partial(combine, plan, chunk),
        out_shape=[shape, shape],
        grid=(nx // chunk,),
        in_specs=[vmem_spec()] * len(operands),
        out_specs=[block, block],
        scratch_shapes=[kept((2 * STEPS + 1, 8, 128))],
        compiler_params=pltpu.CompilerParams(vmem_limit_bytes=40 << 20),
        name="combine",
    )(*[resident(a) for a in operands])
    return out, residual


def solution(mesh):
    placed = P("gx", "gy", "gz")
    return jax.shard_map(
        functools.partial(on_device, mesh),
        mesh=mesh,
        in_specs=(placed,) * 3,
        out_specs=(placed, placed),
        check_vma=False,
    )
```

```python
import functools

import jax
import jax.numpy as jnp
from jax import lax
from jax.experimental import pallas as pl
from jax.experimental.pallas import tpu as pltpu
from jax.sharding import PartitionSpec as P

STEPS = 6
SHIFT = 7.0
GROUPS = 8
WIDE = 16
RIMS = 3
BAND = 40
QUAD = 4
TOP = 8
VMEM = pltpu.VMEM
AXES = ("gx", "gy", "gz")


def vmem_spec():
    return pl.BlockSpec(memory_space=VMEM)


def resident(array):
    return pltpu.with_memory_space_constraint(array, VMEM)


def call(body, outs, name, scratch=(), aliases=None, flops=0):
    return pl.pallas_call(
        body,
        out_shape=outs,
        out_specs=[vmem_spec() for _ in outs],
        scratch_shapes=list(scratch),
        input_output_aliases=aliases or {},
        compiler_params=pltpu.CompilerParams(vmem_limit_bytes=40 << 20),
        cost_estimate=pl.CostEstimate(flops=flops, bytes_accessed=1 << 20, transcendentals=0),
        name=name,
    )


def kept(shape):
    return pltpu.VMEM(shape, jnp.float32)


def lanes(shape=(8, 128)):
    return lax.broadcasted_iota(jnp.int32, shape, len(shape) - 1)


class Plan:
    def __init__(self, mesh, nx, ny, nz):
        self.gx, self.gy, self.gz = (mesh.shape[a] for a in AXES)
        self.nx, self.ny, self.nz = nx, ny, nz
        self.sides = min(self.gx - 1, 2)
        self.planes = nx + STEPS * self.sides
        self.deep = self.planes // GROUPS + 1
        self.rows = ny + 16
        self.half = self.rows // 2
        self.tall = self.rows + 16
        self.rim = self.planes // RIMS + 1

    def own(self):
        if self.sides == 1:
            return lax.axis_index("gx") * STEPS
        return STEPS if self.sides == 2 else 0

    def halo_starts(self):
        if self.sides == 1:
            return [(1 - lax.axis_index("gx")) * self.nx]
        return [0, STEPS + self.nx] if self.sides == 2 else []

    def strips(self):
        parts = [(None, i, STEPS) for i in range(self.nx)]
        for side in range(self.sides):
            for distance in range(1, STEPS):
                toward, away = STEPS - distance, distance - 1
                if self.sides == 1:
                    index = lax.axis_index("gx")
                    plane = index * toward + (1 - index) * away
                else:
                    plane = away if side else toward
                parts.append((side, plane, STEPS - distance))
        return parts

    def strip_rows(self):
        return self.nx * STEPS + self.sides * STEPS * (STEPS - 1) // 2

    def span(self, level):
        if self.sides == 1:
            index = lax.axis_index("gx")
            return level * index, self.planes - level
        cut = level if self.sides == 2 else 0
        return cut, self.planes - 2 * cut


def prepare(plan, rs, inv, act, v_ext, w_ext, *faces):
    own, ny = 1 + plan.own(), plan.ny
    for ext in (v_ext, w_ext):
        ext[...] = jnp.zeros(ext.shape, jnp.float32)
    for i in range(plan.nx):
        liquid = act[i].astype(jnp.float32)
        v_ext[own + i, pl.ds(TOP, ny), :] = rs[i] * liquid
        w_ext[own + i, pl.ds(TOP, ny), :] = inv[i] * liquid * (2.0 / SHIFT)
    if plan.sides == 1:
        starts = [(1 - lax.axis_index("gx")) * (plan.nx - STEPS)]
    else:
        starts = [plan.nx - STEPS, 0]
    for start, face in zip(starts, faces):
        for i in range(STEPS):
            face[0, i] = v_ext[own + start + i, pl.ds(TOP, ny), :]
            face[1, i] = w_ext[own + start + i, pl.ds(TOP, ny), :]


def pack_rows(plan, *refs):
    halos, (v_ext, w_ext, first, second) = refs[2 : 2 + plan.sides], refs[2 + plan.sides :]
    ny = plan.ny
    even = lax.axis_index("gy") % 2 == 0
    starts = plan.halo_starts()
    for field, ext in enumerate((v_ext, w_ext)):
        for start, halo in zip(starts, halos):
            for i in range(STEPS):
                ext[1 + start + i, pl.ds(TOP, ny), :] = halo[field, i]
        offset = 0
        for side, plane, rows in plan.strips():
            at = 1 + plane + (plan.own() if side is None else starts[side])
            low = ext[at, pl.ds(TOP, rows), :]
            high = ext[at, pl.ds(TOP + ny - rows, rows), :]
            first[field, pl.ds(offset, rows), :] = jnp.where(even, high, low)
            second[field, pl.ds(offset, rows), :] = jnp.where(even, low, high)
            offset += rows


def column_block(plan, ext, i, r, group):
    block = jnp.zeros((8, 128), jnp.float32)
    for g in range(GROUPS):
        p = g * plan.deep + i
        if p < plan.planes:
            moved = pltpu.roll(ext[1 + p, pl.ds(8 * r, 8), :], WIDE * g + 8, 1)
            block = jnp.where(group == g, moved, block)
    return block


def rim_block(plan, ext, i, at, band, spot):
    block = jnp.zeros((8, 128), jnp.float32)
    for g in range(RIMS):
        p = g * plan.rim + i
        if p < plan.planes:
            value = ext[1 + p, at, :]
            high = pltpu.roll(value, BAND * g + 12, 1)
            low = pltpu.roll(value, (BAND * g + 28) % 128, 1)
            block = jnp.where((band == g) & (spot < 12), high, block)
            block = jnp.where((band == g) & (spot >= 28), low, block)
    return block


def near(plan, v_ext, w_ext, packed, rim_v, rim_w, *tables):
    inside = range(1, 1 + plan.ny // 8)
    face_tables(w_ext, tables, plan.planes, plan.planes // 2, inside, inside, inside[1:-1])
    group = lanes() // WIDE
    band, spot = lanes() // BAND, lanes() % BAND
    for field, (ext, rim) in enumerate(((v_ext, rim_v), (w_ext, rim_w))):
        for r in inside:
            at = pl.ds(8 * r, 8)
            for i in range(plan.deep):
                packed[field, i, at, :] = column_block(plan, ext, i, r, group)
            for i in range(plan.rim):
                rim[1 + i, at, :] = rim_block(plan, ext, i, at, band, spot)


def pack_lanes(plan, *refs):
    from_first, from_second, packed, v_ext, w_ext, first, second = refs[2:]
    ny = plan.ny
    even_y = lax.axis_index("gy") % 2 == 0
    even_z = lax.axis_index("gz") % 2 == 1
    lane = lanes()
    group = lane // WIDE
    right_half = (lane % WIDE) >= WIDE // 2
    starts = plan.halo_starts()
    last = plan.rows // 8 - 1
    for field, ext in enumerate((v_ext, w_ext)):
        offset = 0
        for side, plane, rows in plan.strips():
            at = 1 + plane + (plan.own() if side is None else starts[side])
            one = from_first[field, pl.ds(offset, rows), :]
            two = from_second[field, pl.ds(offset, rows), :]
            ext[at, pl.ds(TOP - rows, rows), :] = jnp.where(even_y, two, one)
            ext[at, pl.ds(TOP + ny, rows), :] = jnp.where(even_y, one, two)
            offset += rows
    for field, ext in enumerate((v_ext, w_ext)):
        for i in range(plan.deep):
            blocks = [packed[field, i, pl.ds(8 * r, 8), :] for r in range(1, last)]
            blocks = [column_block(plan, ext, i, 0, group)] + blocks
            blocks = blocks + [column_block(plan, ext, i, last, group)]
            for r in range(plan.half // 8):
                upper, lower = blocks[r], blocks[plan.half // 8 + r]
                to_right = jnp.where(right_half, pltpu.roll(lower, 8, 1), upper)
                to_left = jnp.where(right_half, lower, pltpu.roll(upper, 120, 1))
                first[field, i, pl.ds(8 * r, 8), :] = jnp.where(even_z, to_right, to_left)
                second[field, i, pl.ds(8 * r, 8), :] = jnp.where(even_z, to_left, to_right)


def coupling(one, two):
    total = jnp.maximum(one + two, 0.0625)
    inverse = pl.reciprocal(total, approx=True)
    inverse = inverse * (2.0 - total * inverse)
    return (one * two) * inverse


def face_tables(weight, tables, planes, unroll, across, along, diagonals):
    cx, cy, cz, dg = tables

    for r in across:
        at = pl.ds(8 * r, 8)
        cx[0, at, :] = coupling(weight[0, at, :], weight[1, at, :])

    def faces(trip, _):
        for u in range(unroll):
            p = 1 + unroll * trip + u
            for r in sorted({*across, *along}):
                at = pl.ds(8 * r, 8)
                here = weight[p, at, :]
                if r in across:
                    cx[p, at, :] = coupling(here, weight[p + 1, at, :])
                    cz[p, at, :] = coupling(here, pltpu.roll(here, 127, 1))
                if r in along:
                    below = weight[p, pl.ds(8 * r + 1, 8), :]
                    cy[p, pl.ds(8 * r + 8, 8), :] = coupling(here, below)
        return 0

    lax.fori_loop(0, planes // unroll, faces, 0)

    def diagonal(trip, _):
        for u in range(unroll):
            p = 1 + unroll * trip + u
            for r in diagonals:
                at = pl.ds(8 * r, 8)
                air = 0.5 * weight[p, at, :]
                total = jnp.full((8, 128), -1.0, jnp.float32)
                ahead = cz[p, at, :]
                for face in (
                    cx[p, at, :],
                    cx[p - 1, at, :],
                    cy[p, pl.ds(8 * r + 8, 8), :],
                    cy[p, pl.ds(8 * r + 7, 8), :],
                    ahead,
                    pltpu.roll(ahead, 1, 1),
                ):
                    total = total + jnp.where(face > 0.0, face, air)
                dg[p, at, :] = total
        return 0

    lax.fori_loop(0, planes // unroll, diagonal, 0)


def advance(source, target, tables, first, trips, unroll, start, blocks):
    cx, cy, cz, dg = tables

    def body(trip, _):
        base = first + trip * unroll
        for u0, r in [(u0, r) for u0 in range(0, unroll, QUAD) for r in range(blocks)]:
            s = start + 8 * r
            at = pl.ds(s, 8)
            top = min(u0 + QUAD, unroll)
            fields = {u: source[base + u, at, :] for u in range(u0, top + 2)}
            walls = {u: cx[base + u, at, :] for u in range(u0, top + 1)}
            for u in range(u0, top):
                p = base + u + 1
                here, ahead = fields[u + 1], cz[p, at, :]
                after = pltpu.roll(here, 127, 1)
                behind = pltpu.roll(ahead * here, 1, 1)
                total = walls[u + 1] * fields[u + 2] + walls[u] * fields[u]
                total = total + cy[p, pl.ds(s + 8, 8), :] * source[p, pl.ds(s + 1, 8), :]
                total = total + cy[p, pl.ds(s + 7, 8), :] * source[p, pl.ds(s - 1, 8), :]
                total = total + (ahead * after + behind)
                target[p, at, :] = dg[p, at, :] * here - total
        return 0

    lax.fori_loop(0, trips, body, 0)


def level_rows(plan, level):
    return TOP - STEPS + level, -(-(plan.ny + 2 * (STEPS - level)) // 8)


def products(fields, sums):
    for k in range(STEPS + 1):
        sums[2 * k] = sums[2 * k] + fields[k] * fields[k]
        if k < STEPS:
            sums[2 * k + 1] = sums[2 * k + 1] + fields[k] * fields[k + 1]
    return sums


def inner(plan, *refs):
    v_ext, w_ext = refs[:2]
    basis, (sums_ref, rim_v, rim_w), tables = refs[8 : 8 + STEPS], refs[8 + STEPS : -4], refs[-4:]
    planes = plan.planes
    blank8 = jnp.zeros((8, 128), jnp.float32)
    last = plan.rows // 8 - 1
    halo = (0, last)
    face_tables(w_ext, tables, planes, planes // 2, halo, (0, last - 1, last), (0, 1, last - 1, last))
    for ref in basis:
        ref[0] = jnp.zeros(ref.shape[1:], jnp.float32)
        ref[planes + 1] = jnp.zeros(ref.shape[1:], jnp.float32)
    source = v_ext
    for level in range(1, STEPS + 1):
        low, count = plan.span(level)
        trips = 2
        unroll = -(-count // trips)
        low = jnp.minimum(low, planes - unroll * trips)
        start, blocks = level_rows(plan, level)
        advance(source, basis[level - 1], tables, low, trips, unroll, start, blocks)
        source = basis[level - 1]

    own = 1 + plan.own()

    def gather(p, sums):
        sums = list(sums)
        for r in range(plan.ny // 8):
            at = pl.ds(TOP + 8 * r, 8)
            sums = products([ref[own + p, at, :] for ref in (v_ext,) + tuple(basis)], sums)
        return tuple(sums)

    sums = lax.fori_loop(0, plan.nx, gather, (blank8,) * (2 * STEPS + 1))
    lane = lanes()
    fresh = (lane >= STEPS) & (lane < 128 - STEPS)
    for j, part in enumerate(sums):
        sums_ref[j] = jnp.where(fresh, part, 0.0)

    band, spot = lane // BAND, lane % BAND
    for ext, rim in ((v_ext, rim_v), (w_ext, rim_w)):
        for r in halo:
            at = pl.ds(8 * r, 8)
            for i in range(plan.rim):
                rim[1 + i, at, :] = rim_block(plan, ext, i, at, band, spot)


def outer(plan, first, second, rim_v, rim_w, sums_ref, *refs):
    basis, (moments, rim_0, rim_s), tables = refs[:STEPS], refs[STEPS : STEPS + 3], refs[STEPS + 3 :]
    planes, deep, half, rim = plan.planes, plan.deep, plan.half, plan.rim
    even_z = lax.axis_index("gz") % 2 == 1
    lane = lanes()
    right_half = (lane % WIDE) >= WIDE // 2
    band, spot = lane // BAND, lane % BAND
    halo = (spot >= 12) & (spot < 28)
    blank8 = jnp.zeros((8, 128), jnp.float32)

    def wrap(ref, start, blocks):
        for r in range(blocks):
            at = pl.ds(start + 8 * r, 8)
            ref[0, at, :] = pltpu.roll(ref[rim, at, :], BAND, 1)
            ref[rim + 1, at, :] = pltpu.roll(ref[1, at, :], 128 - BAND, 1)

    for field, (own, full) in enumerate(((rim_v, rim_0), (rim_w, rim_s))):
        columns = [[None] * (2 * (half // 8)) for _ in range(deep)]
        for i in range(deep):
            for r in range(half // 8):
                one = first[field, i, pl.ds(8 * r, 8), :]
                two = second[field, i, pl.ds(8 * r, 8), :]
                left = jnp.where(even_z, two, one)
                right = jnp.where(even_z, one, two)
                columns[i][r] = jnp.where(right_half, pltpu.roll(left, 8, 1), right)
                columns[i][half // 8 + r] = jnp.where(right_half, left, pltpu.roll(right, 120, 1))
        for r in range(plan.rows // 8):
            at = pl.ds(8 * r, 8)
            for i in range(rim):
                block = own[1 + i, at, :]
                for g in range(RIMS):
                    p = g * rim + i
                    if p < planes:
                        turn = (BAND * g + 12 - WIDE * (p // deep)) % 128
                        moved = pltpu.roll(columns[p % deep][r], turn, 1)
                        block = jnp.where((band == g) & halo, moved, block)
                full[1 + i, at, :] = block
        for i in range(rim + 2):
            full[i, pl.ds(plan.rows, 16), :] = jnp.zeros((16, 128), jnp.float32)
        wrap(full, 0, plan.rows // 8)

    every = range(plan.rows // 8)
    face_tables(rim_s, tables, rim, rim, every, every, every)
    source = rim_0
    for level in range(1, STEPS + 1):
        start, blocks = level_rows(plan, level)
        advance(source, basis[level - 1], tables, 0, 1, rim, start, blocks)
        source = basis[level - 1]
        if level < STEPS:
            wrap(source, start, blocks)

    own = plan.own()
    fresh = ((spot >= 6) & (spot < 12)) | ((spot >= 28) & (spot < 34))
    sums = [sums_ref[j] for j in range(2 * STEPS + 1)]
    for i in range(rim):
        part = [blank8] * (2 * STEPS + 1)
        for r in range(plan.ny // 8):
            at = pl.ds(TOP + 8 * r, 8)
            part = products([ref[1 + i, at, :] for ref in (rim_0,) + tuple(basis)], part)
        plane = band * rim + i
        mine = fresh & (plane >= own) & (plane < own + plan.nx)
        sums = [a + jnp.where(mine, b, 0.0) for a, b in zip(sums, part)]
    line = jnp.zeros((1, 128), jnp.float32)
    for j, part in enumerate(sums):
        line = jnp.where(lanes((1, 128)) == j, jnp.sum(part), line)
    for j in range(moments.shape[0]):
        moments[j] = line


def weigh(parts):
    line = jnp.sum(parts, axis=0)
    line = jnp.broadcast_to(line, (8, 128))
    moment = []
    for j in range(2 * STEPS + 1):
        picked = jnp.where(lanes() == j, line, 0.0)
        moment.append(jnp.broadcast_to(jnp.sum(picked, axis=1, keepdims=True), (8, 128)))
    count = STEPS + 1
    gram = [[moment[i + j] for j in range(count)] for i in range(count)]
    sign = [1.0 if k % 2 == 0 else -1.0 for k in range(count)]
    rhs = [jnp.full((8, 128), s, jnp.float32) for s in sign]
    inverse = []
    for p in range(count):
        inverse.append(1.0 / gram[p][p])
        for i in range(p + 1, count):
            factor = gram[p][i] * inverse[p]
            for j in range(i, count):
                gram[i][j] = gram[i][j] - factor * gram[p][j]
            rhs[i] = rhs[i] - factor * rhs[p]
    solved = [None] * count
    for p in reversed(range(count)):
        running = rhs[p]
        for j in range(p + 1, count):
            running = running - gram[p][j] * solved[j]
        solved[p] = running * inverse[p]
    scale = sign[0] * solved[0]
    for k in range(1, count):
        scale = scale + sign[k] * solved[k]
    scale = 1.0 / scale
    leftover = [s * scale for s in solved]
    coefficients = [(1.0 - leftover[0]) * (1.0 / SHIFT)]
    for k in range(1, STEPS):
        coefficients.append(leftover[k] * (-1.0 / SHIFT) - coefficients[-1])
    return coefficients, leftover


def combine(plan, chunk, parts, v_ext, rim_0, *refs):
    basis, rims = refs[:STEPS], refs[STEPS : 2 * STEPS]
    solution_field, residual, weights = refs[2 * STEPS :]

    @pl.when(pl.program_id(0) == 0)
    def _():
        coefficients, leftover = weigh(parts[...])
        for k, value in enumerate(coefficients + leftover):
            weights[k] = value

    own = plan.own() + pl.program_id(0) * chunk
    lane = lanes()

    def mix(refs, p, at):
        fields = [ref[p, at, :] for ref in refs]
        one, two = weights[0] * fields[0], weights[STEPS] * fields[0]
        for k in range(1, STEPS):
            one = one + weights[k] * fields[k]
            two = two + weights[STEPS + k] * fields[k]
        return one, two + weights[2 * STEPS] * fields[STEPS]

    for p in range(chunk):
        plane = own + p
        band = plane // plan.rim
        depth = plane - band * plan.rim
        low = 100 - BAND * band
        low = jnp.where(low < 0, low + 128, low)
        high = 116 - BAND * band
        for r in range(plan.ny // 8):
            at = pl.ds(TOP + 8 * r, 8)
            mains = mix((v_ext,) + tuple(basis), 1 + plane, at)
            edges = mix((rim_0,) + tuple(rims), 1 + depth, at)
            for out, main, edge in zip((solution_field, residual), mains, edges):
                value = jnp.where(lane < STEPS, pltpu.roll(edge, low, 1), main)
                value = jnp.where(lane >= 128 - STEPS, pltpu.roll(edge, high, 1), value)
                out[p, pl.ds(8 * r, 8), :] = value


def swaps(first, second, axis):
    count = lax.axis_size(axis)
    starts = (0, 1) if axis == "gy" else (1, 0)
    ones, twos = ([(i, i + 1) for i in range(s, count - 1, 2)] for s in starts)
    return tuple(
        lax.ppermute(value, axis, pairs + [(b, a) for a, b in pairs])
        for value, pairs in ((first, ones), (second, twos))
    )


def on_device(mesh, right_side, inv_density, active):
    nx, ny, nz = right_side.shape
    plan = Plan(mesh, nx, ny, nz)
    table = kept((plan.planes + 2, plan.tall, 128))
    face = kept((2, STEPS, ny, nz))
    inputs = [
        pltpu.with_memory_space_constraint(a, pltpu.HBM) for a in (right_side, inv_density, active)
    ]
    v_ext, w_ext, *faces = call(
        functools.partial(prepare, plan), [table, table] + [face] * plan.sides, "prepare"
    )(*inputs)
    if plan.sides == 1:
        halos = [lax.ppermute(faces[0], "gx", [(0, 1), (1, 0)])]
    else:
        steps = [(i, i + 1) for i in range(plan.gx - 1)]
        pairs = [steps, [(b, a) for a, b in steps]]
        halos = [lax.ppermute(f, "gx", p) for f, p in zip(faces, pairs)]
    strip = kept((2, plan.strip_rows(), 128))
    v_ext, w_ext, first, second = call(
        functools.partial(pack_rows, plan), [table, table, strip, strip], "rows", aliases={0: 0, 1: 1}
    )(*[resident(a) for a in (v_ext, w_ext, *halos)])
    first, second = swaps(first, second, "gy")
    rim = kept((plan.rim + 2, plan.tall, 128))
    packed, rim_v, rim_w, *tables = call(
        functools.partial(near, plan),
        [kept((2, plan.deep, plan.rows, 128)), rim, rim] + [table] * 4,
        "near",
        flops=1 << 24,
    )(resident(v_ext), resident(w_ext))
    column = kept((2, plan.deep, plan.half, 128))
    v_ext, w_ext, first, second = call(
        functools.partial(pack_lanes, plan),
        [table, table, column, column],
        "columns",
        aliases={0: 0, 1: 1},
    )(*[resident(a) for a in (v_ext, w_ext, first, second, packed)])
    first, second = swaps(first, second, "gz")
    v_ext, w_ext = resident(v_ext), resident(w_ext)
    devices = plan.gx * plan.gy * plan.gz
    sums = kept((2 * STEPS + 1, 8, 128))
    *basis, sums, rim_v, rim_w = call(
        functools.partial(inner, plan),
        [table] * STEPS + [sums, rim, rim] + [table] * 4,
        "inner",
        aliases={i: i + STEPS - 1 for i in range(2, 8)},
        flops=1 << 24,
    )(v_ext, w_ext, *[resident(a) for a in (rim_v, rim_w, *tables)])[: STEPS + 3]
    *rims, moments, rim_0 = call(
        functools.partial(outer, plan),
        [rim] * STEPS + [kept((devices, 1, 128)), rim],
        "outer",
        scratch=[rim] * 5,
    )(*[resident(a) for a in (first, second, rim_v, rim_w, sums)])
    parts = lax.all_to_all(moments, AXES, 0, 0, tiled=True)
    chunk = 4
    block = pl.BlockSpec((chunk, ny, nz), lambda i: (i, 0, 0))
    shape = jax.ShapeDtypeStruct((nx, ny, nz), jnp.float32)
    operands = [parts, v_ext, rim_0] + basis + rims
    out, residual = pl.pallas_call(
        functools.partial(combine, plan, chunk),
        out_shape=[shape, shape],
        grid=(nx // chunk,),
        in_specs=[vmem_spec()] * len(operands),
        out_specs=[block, block],
        scratch_shapes=[kept((2 * STEPS + 1, 8, 128))],
        compiler_params=pltpu.CompilerParams(vmem_limit_bytes=40 << 20),
        name="combine",
    )(*[resident(a) for a in operands])
    return out, residual


def solution(mesh):
    placed = P("gx", "gy", "gz")
    return jax.shard_map(
        functools.partial(on_device, mesh),
        mesh=mesh,
        in_specs=(placed,) * 3,
        out_specs=(placed, placed),
        check_vma=False,
    )
```

```python
import functools

import jax
import jax.numpy as jnp
from jax import lax
from jax.experimental import pallas as pl
from jax.experimental.pallas import tpu as pltpu
from jax.sharding import PartitionSpec as P

STEPS = 6
SHIFT = 7.0
GROUPS = 8
WIDE = 16
RIMS = 3
BAND = 40
EARLY = 4
QUAD = 4
TOP = 8
VMEM = pltpu.VMEM
AXES = ("gx", "gy", "gz")


def vmem_spec():
    return pl.BlockSpec(memory_space=VMEM)


def resident(array):
    return pltpu.with_memory_space_constraint(array, VMEM)


def call(body, outs, name, scratch=(), aliases=None, flops=0):
    return pl.pallas_call(
        body,
        out_shape=outs,
        out_specs=[vmem_spec() for _ in outs],
        scratch_shapes=list(scratch),
        input_output_aliases=aliases or {},
        compiler_params=pltpu.CompilerParams(vmem_limit_bytes=40 << 20),
        cost_estimate=pl.CostEstimate(flops=flops, bytes_accessed=1 << 20, transcendentals=0),
        name=name,
    )


def kept(shape):
    return pltpu.VMEM(shape, jnp.float32)


def lanes(shape=(8, 128)):
    return lax.broadcasted_iota(jnp.int32, shape, len(shape) - 1)


class Plan:
    def __init__(self, mesh, nx, ny, nz):
        self.gx, self.gy, self.gz = (mesh.shape[a] for a in AXES)
        self.nx, self.ny, self.nz = nx, ny, nz
        self.sides = min(self.gx - 1, 2)
        self.planes = nx + STEPS * self.sides
        self.deep = self.planes // GROUPS + 1
        self.rows = ny + 16
        self.half = self.rows // 2
        self.tall = self.rows + 16
        self.rim = self.planes // RIMS + 1

    def own(self):
        if self.sides == 1:
            return lax.axis_index("gx") * STEPS
        return STEPS if self.sides == 2 else 0

    def halo_starts(self):
        if self.sides == 1:
            return [(1 - lax.axis_index("gx")) * self.nx]
        return [0, STEPS + self.nx] if self.sides == 2 else []

    def strips(self):
        parts = [(None, i, STEPS) for i in range(self.nx)]
        for side in range(self.sides):
            for distance in range(1, STEPS):
                toward, away = STEPS - distance, distance - 1
                if self.sides == 1:
                    index = lax.axis_index("gx")
                    plane = index * toward + (1 - index) * away
                else:
                    plane = away if side else toward
                parts.append((side, plane, STEPS - distance))
        return parts

    def strip_rows(self):
        return self.nx * STEPS + self.sides * STEPS * (STEPS - 1) // 2

    def span(self, level):
        if self.sides == 1:
            index = lax.axis_index("gx")
            return level * index, self.planes - level
        cut = level if self.sides == 2 else 0
        return cut, self.planes - 2 * cut


def prepare(plan, rs, inv, act, v_ext, w_ext, *faces):
    own, ny = 1 + plan.own(), plan.ny
    for ext in (v_ext, w_ext):
        ext[...] = jnp.zeros(ext.shape, jnp.float32)
    for i in range(plan.nx):
        liquid = act[i].astype(jnp.float32)
        v_ext[own + i, pl.ds(TOP, ny), :] = rs[i] * liquid
        w_ext[own + i, pl.ds(TOP, ny), :] = inv[i] * liquid * (2.0 / SHIFT)
    if plan.sides == 1:
        starts = [(1 - lax.axis_index("gx")) * (plan.nx - STEPS)]
    else:
        starts = [plan.nx - STEPS, 0]
    for start, face in zip(starts, faces):
        for i in range(STEPS):
            face[0, i] = v_ext[own + start + i, pl.ds(TOP, ny), :]
            face[1, i] = w_ext[own + start + i, pl.ds(TOP, ny), :]


def pack_rows(plan, *refs):
    halos, (v_ext, w_ext, first, second) = refs[2 : 2 + plan.sides], refs[2 + plan.sides :]
    ny = plan.ny
    even = lax.axis_index("gy") % 2 == 0
    starts = plan.halo_starts()
    for field, ext in enumerate((v_ext, w_ext)):
        for start, halo in zip(starts, halos):
            for i in range(STEPS):
                ext[1 + start + i, pl.ds(TOP, ny), :] = halo[field, i]
        offset = 0
        for side, plane, rows in plan.strips():
            at = 1 + plane + (plan.own() if side is None else starts[side])
            low = ext[at, pl.ds(TOP, rows), :]
            high = ext[at, pl.ds(TOP + ny - rows, rows), :]
            first[field, pl.ds(offset, rows), :] = jnp.where(even, high, low)
            second[field, pl.ds(offset, rows), :] = jnp.where(even, low, high)
            offset += rows


def column_block(plan, ext, i, r, group):
    block = jnp.zeros((8, 128), jnp.float32)
    for g in range(GROUPS):
        p = g * plan.deep + i
        if p < plan.planes:
            moved = pltpu.roll(ext[1 + p, pl.ds(8 * r, 8), :], WIDE * g + 8, 1)
            block = jnp.where(group == g, moved, block)
    return block


def rim_block(plan, ext, i, at, band, spot):
    block = jnp.zeros((8, 128), jnp.float32)
    for g in range(RIMS):
        p = g * plan.rim + i
        if p < plan.planes:
            value = ext[1 + p, at, :]
            high = pltpu.roll(value, BAND * g + 12, 1)
            low = pltpu.roll(value, (BAND * g + 28) % 128, 1)
            block = jnp.where((band == g) & (spot < 12), high, block)
            block = jnp.where((band == g) & (spot >= 28), low, block)
    return block


def near(plan, v_ext, w_ext, packed, rim_v, rim_w, *refs):
    tables, basis = refs[:4], refs[4:]
    planes = plan.planes
    inside = range(1, 1 + plan.ny // 8)
    for p in range(planes + 2):
        tables[1][p, pl.ds(TOP, 8), :] = jnp.zeros((8, 128), jnp.float32)
    face_tables(w_ext, tables, planes, planes // 2, inside, inside, inside)
    group = lanes() // WIDE
    band, spot = lanes() // BAND, lanes() % BAND
    for field, (ext, rim) in enumerate(((v_ext, rim_v), (w_ext, rim_w))):
        for r in inside:
            at = pl.ds(8 * r, 8)
            for i in range(plan.deep):
                packed[field, i, at, :] = column_block(plan, ext, i, r, group)
            for i in range(plan.rim):
                rim[1 + i, at, :] = rim_block(plan, ext, i, at, band, spot)
    for ref in basis:
        ref[0] = jnp.zeros(ref.shape[1:], jnp.float32)
        ref[planes + 1] = jnp.zeros(ref.shape[1:], jnp.float32)
    source = v_ext
    for level in range(1, EARLY + 1):
        sweep(plan, level, source, basis[level - 1], tables, [8 * r for r in inside])
        source = basis[level - 1]


def pack_lanes(plan, *refs):
    from_first, from_second, packed, v_ext, w_ext, first, second = refs[2:]
    ny = plan.ny
    even_y = lax.axis_index("gy") % 2 == 0
    even_z = lax.axis_index("gz") % 2 == 1
    lane = lanes()
    group = lane // WIDE
    right_half = (lane % WIDE) >= WIDE // 2
    starts = plan.halo_starts()
    last = plan.rows // 8 - 1
    for field, ext in enumerate((v_ext, w_ext)):
        offset = 0
        for side, plane, rows in plan.strips():
            at = 1 + plane + (plan.own() if side is None else starts[side])
            one = from_first[field, pl.ds(offset, rows), :]
            two = from_second[field, pl.ds(offset, rows), :]
            ext[at, pl.ds(TOP - rows, rows), :] = jnp.where(even_y, two, one)
            ext[at, pl.ds(TOP + ny, rows), :] = jnp.where(even_y, one, two)
            offset += rows
    for field, ext in enumerate((v_ext, w_ext)):
        for i in range(plan.deep):
            blocks = [packed[field, i, pl.ds(8 * r, 8), :] for r in range(1, last)]
            blocks = [column_block(plan, ext, i, 0, group)] + blocks
            blocks = blocks + [column_block(plan, ext, i, last, group)]
            for r in range(plan.half // 8):
                upper, lower = blocks[r], blocks[plan.half // 8 + r]
                to_right = jnp.where(right_half, pltpu.roll(lower, 8, 1), upper)
                to_left = jnp.where(right_half, lower, pltpu.roll(upper, 120, 1))
                first[field, i, pl.ds(8 * r, 8), :] = jnp.where(even_z, to_right, to_left)
                second[field, i, pl.ds(8 * r, 8), :] = jnp.where(even_z, to_left, to_right)


def coupling(one, two):
    total = jnp.maximum(one + two, 0.0625)
    inverse = pl.reciprocal(total, approx=True)
    inverse = inverse * (2.0 - total * inverse)
    return (one * two) * inverse


def face_tables(weight, tables, planes, unroll, across, along, diagonals):
    cx, cy, cz, dg = tables

    for r in across:
        at = pl.ds(8 * r, 8)
        cx[0, at, :] = coupling(weight[0, at, :], weight[1, at, :])

    def faces(trip, _):
        for u in range(unroll):
            p = 1 + unroll * trip + u
            for r in sorted({*across, *along}):
                at = pl.ds(8 * r, 8)
                here = weight[p, at, :]
                if r in across:
                    cx[p, at, :] = coupling(here, weight[p + 1, at, :])
                    cz[p, at, :] = coupling(here, pltpu.roll(here, 127, 1))
                if r in along:
                    below = weight[p, pl.ds(8 * r + 1, 8), :]
                    cy[p, pl.ds(8 * r + 8, 8), :] = coupling(here, below)
        return 0

    lax.fori_loop(0, planes // unroll, faces, 0)

    def diagonal(trip, _):
        for u in range(unroll):
            p = 1 + unroll * trip + u
            for r in diagonals:
                at = pl.ds(8 * r, 8)
                air = 0.5 * weight[p, at, :]
                total = jnp.full((8, 128), -1.0, jnp.float32)
                ahead = cz[p, at, :]
                for face in (
                    cx[p, at, :],
                    cx[p - 1, at, :],
                    cy[p, pl.ds(8 * r + 8, 8), :],
                    cy[p, pl.ds(8 * r + 7, 8), :],
                    ahead,
                    pltpu.roll(ahead, 1, 1),
                ):
                    total = total + jnp.where(face > 0.0, face, air)
                dg[p, at, :] = total
        return 0

    lax.fori_loop(0, planes // unroll, diagonal, 0)


def advance(source, target, tables, first, trips, unroll, starts):
    cx, cy, cz, dg = tables

    def body(trip, _):
        base = first + trip * unroll
        for u0, s in [(u0, s) for u0 in range(0, unroll, QUAD) for s in starts]:
            at = pl.ds(s, 8)
            top = min(u0 + QUAD, unroll)
            fields = {u: source[base + u, at, :] for u in range(u0, top + 2)}
            walls = {u: cx[base + u, at, :] for u in range(u0, top + 1)}
            for u in range(u0, top):
                p = base + u + 1
                here, ahead = fields[u + 1], cz[p, at, :]
                after = pltpu.roll(here, 127, 1)
                behind = pltpu.roll(ahead * here, 1, 1)
                total = walls[u + 1] * fields[u + 2] + walls[u] * fields[u]
                total = total + cy[p, pl.ds(s + 8, 8), :] * source[p, pl.ds(s + 1, 8), :]
                total = total + cy[p, pl.ds(s + 7, 8), :] * source[p, pl.ds(s - 1, 8), :]
                total = total + (ahead * after + behind)
                target[p, at, :] = dg[p, at, :] * here - total
        return 0

    if trips == 1:
        body(0, 0)
    else:
        lax.fori_loop(0, trips, body, 0)


def march(source, target, tables, first, trips, unroll, starts):
    cx, cy, cz, dg = tables
    row = lax.broadcasted_iota(jnp.int32, (8, 128), 0)
    top_row, end_row = row == 0, row == 7

    def body(trip, _):
        base = first + trip * unroll
        for u0 in range(0, unroll, QUAD):
            here = {u: None for u in range(u0, min(u0 + QUAD, unroll))}
            lifted, passed = {}, {}
            for s in starts:
                at, beyond = pl.ds(s, 8), pl.ds(s + 8, 8)
                for u in here:
                    p = base + u + 1
                    if s == starts[0]:
                        here[u] = source[p, at, :]
                        lifted[u] = pltpu.roll(here[u], 7, 0)
                        if s:
                            previous = cy[p, at, :] * source[p, pl.ds(s - 8, 8), :]
                            passed[u] = pltpu.roll(previous, 1, 0)
                fields = {u + 1: value for u, value in here.items()}
                fields[u0] = source[base + u0, at, :]
                final = max(here)
                fields[final + 2] = source[base + final + 2, at, :]
                walls = {u: cx[base + u, at, :] for u in range(u0, final + 2)}
                for u in here:
                    p = base + u + 1
                    value, ahead = here[u], cz[p, at, :]
                    wall = cy[p, beyond, :]
                    after = pltpu.roll(value, 127, 1)
                    behind = pltpu.roll(ahead * value, 1, 1)
                    sunk = pltpu.roll(wall * value, 1, 0)
                    upper = jnp.where(top_row, passed.get(u, sunk), sunk)
                    passed[u] = sunk
                    here[u] = source[p, beyond, :]
                    rising = pltpu.roll(here[u], 7, 0)
                    lower = jnp.where(end_row, rising, lifted[u])
                    lifted[u] = rising
                    total = walls[u + 1] * fields[u + 2] + walls[u] * fields[u]
                    total = total + (wall * lower + upper)
                    total = total + (ahead * after + behind)
                    target[p, at, :] = dg[p, at, :] * value - total
        return 0

    if trips == 1:
        body(0, 0)
    else:
        lax.fori_loop(0, trips, body, 0)


def sweep(plan, level, source, target, tables, starts):
    low, count = plan.span(level)
    half = -(-count // 2)
    low = jnp.minimum(low, plan.planes - 2 * half)
    march(source, target, tables, low, 2, half, starts)


def level_rows(plan, level):
    return range(0, plan.rows, 8) if level < STEPS else range(TOP, TOP + plan.ny, 8)


def products(fields, sums):
    for k in range(STEPS + 1):
        sums[2 * k] = sums[2 * k] + fields[k] * fields[k]
        if k < STEPS:
            sums[2 * k + 1] = sums[2 * k + 1] + fields[k] * fields[k + 1]
    return sums


def inner(plan, *refs):
    v_ext, w_ext = refs[:2]
    sums_ref, rim_v, rim_w, *refs = refs[8 + STEPS :]
    tables, basis = refs[:4], refs[4:]
    planes = plan.planes
    blank8 = jnp.zeros((8, 128), jnp.float32)
    last = plan.rows // 8 - 1
    halo = (0, last)
    face_tables(w_ext, tables, planes, planes // 2, halo, (0, last - 1, last), (0, 1, last - 1, last))
    source = v_ext
    for level in range(1, STEPS + 1):
        if level <= EARLY:
            low, count = plan.span(level)
            starts = [TOP - STEPS + level, TOP + plan.ny - 2 - level]
            advance(source, basis[level - 1], tables, low, 1, count, starts)
        else:
            sweep(plan, level, source, basis[level - 1], tables, level_rows(plan, level))
        source = basis[level - 1]

    own = 1 + plan.own()

    def gather(p, sums):
        sums = list(sums)
        for r in range(plan.ny // 8):
            at = pl.ds(TOP + 8 * r, 8)
            sums = products([ref[own + p, at, :] for ref in (v_ext,) + tuple(basis)], sums)
        return tuple(sums)

    sums = lax.fori_loop(0, plan.nx, gather, (blank8,) * (2 * STEPS + 1))
    lane = lanes()
    fresh = (lane >= STEPS) & (lane < 128 - STEPS)
    for j, part in enumerate(sums):
        sums_ref[j] = jnp.where(fresh, part, 0.0)

    band, spot = lane // BAND, lane % BAND
    for ext, rim in ((v_ext, rim_v), (w_ext, rim_w)):
        for r in halo:
            at = pl.ds(8 * r, 8)
            for i in range(plan.rim):
                rim[1 + i, at, :] = rim_block(plan, ext, i, at, band, spot)


def outer(plan, first, second, rim_v, rim_w, sums_ref, *refs):
    levels, moments, rim_s, *tables = refs
    rim_0, *basis = [levels.at[k] for k in range(STEPS + 1)]
    planes, deep, half, rim = plan.planes, plan.deep, plan.half, plan.rim
    even_z = lax.axis_index("gz") % 2 == 1
    lane = lanes()
    right_half = (lane % WIDE) >= WIDE // 2
    band, spot = lane // BAND, lane % BAND
    halo = (spot >= 12) & (spot < 28)
    blank8 = jnp.zeros((8, 128), jnp.float32)

    def wrap(ref, starts):
        for start in starts:
            at = pl.ds(start, 8)
            ref[0, at, :] = pltpu.roll(ref[rim, at, :], BAND, 1)
            ref[rim + 1, at, :] = pltpu.roll(ref[1, at, :], 128 - BAND, 1)

    for field, (own, full) in enumerate(((rim_v, rim_0), (rim_w, rim_s))):
        columns = [[None] * (2 * (half // 8)) for _ in range(deep)]
        for i in range(deep):
            for r in range(half // 8):
                one = first[field, i, pl.ds(8 * r, 8), :]
                two = second[field, i, pl.ds(8 * r, 8), :]
                left = jnp.where(even_z, two, one)
                right = jnp.where(even_z, one, two)
                columns[i][r] = jnp.where(right_half, pltpu.roll(left, 8, 1), right)
                columns[i][half // 8 + r] = jnp.where(right_half, left, pltpu.roll(right, 120, 1))
        for r in range(plan.rows // 8):
            at = pl.ds(8 * r, 8)
            for i in range(rim):
                block = own[1 + i, at, :]
                for g in range(RIMS):
                    p = g * rim + i
                    if p < planes:
                        turn = (BAND * g + 12 - WIDE * (p // deep)) % 128
                        moved = pltpu.roll(columns[p % deep][r], turn, 1)
                        block = jnp.where((band == g) & halo, moved, block)
                full[1 + i, at, :] = block
        for i in range(rim + 2):
            full[i, pl.ds(plan.rows, 16), :] = jnp.zeros((16, 128), jnp.float32)
        wrap(full, range(0, plan.rows, 8))

    every = range(plan.rows // 8)
    face_tables(rim_s, tables, rim, rim, every, every, every)
    source = rim_0
    for level in range(1, STEPS + 1):
        starts = level_rows(plan, level)
        target = basis[level - 1]
        march(source, target, tables, 0, 1, 1, starts)
        march(source, target, tables, rim - 1, 1, 1, starts)
        if level < STEPS:
            wrap(target, starts)
        march(source, target, tables, 1, 1, rim - 2, starts)
        source = target

    own = plan.own()
    fresh = ((spot >= 6) & (spot < 12)) | ((spot >= 28) & (spot < 34))
    sums = [sums_ref[j] for j in range(2 * STEPS + 1)]
    for i in range(rim):
        part = [blank8] * (2 * STEPS + 1)
        for r in range(plan.ny // 8):
            at = pl.ds(TOP + 8 * r, 8)
            part = products([ref[1 + i, at, :] for ref in (rim_0,) + tuple(basis)], part)
        plane = band * rim + i
        mine = fresh & (plane >= own) & (plane < own + plan.nx)
        sums = [a + jnp.where(mine, b, 0.0) for a, b in zip(sums, part)]
    row = lax.broadcasted_iota(jnp.int32, (16, 128), 0)
    stacked = jnp.zeros((16, 128), jnp.float32)
    for j, part in enumerate(sums):
        stacked = jnp.where(row == j, jnp.sum(part, axis=0, keepdims=True), stacked)
    stacked = jnp.sum(stacked, axis=1, keepdims=True)
    line = jnp.sum(jnp.where(lanes((16, 128)) == row, stacked, 0.0), axis=0, keepdims=True)
    for j in range(moments.shape[0]):
        moments[j] = line


def weigh(parts):
    line = jnp.sum(parts, axis=0)
    line = jnp.broadcast_to(line, (8, 128))
    moment = []
    for j in range(2 * STEPS + 1):
        picked = jnp.where(lanes() == j, line, 0.0)
        moment.append(jnp.broadcast_to(jnp.sum(picked, axis=1, keepdims=True), (8, 128)))
    count = STEPS + 1
    gram = [[moment[i + j] for j in range(count)] for i in range(count)]
    sign = [1.0 if k % 2 == 0 else -1.0 for k in range(count)]
    rhs = [jnp.full((8, 128), s, jnp.float32) for s in sign]
    inverse = []
    for p in range(count):
        inverse.append(1.0 / gram[p][p])
        for i in range(p + 1, count):
            factor = gram[p][i] * inverse[p]
            for j in range(i, count):
                gram[i][j] = gram[i][j] - factor * gram[p][j]
            rhs[i] = rhs[i] - factor * rhs[p]
    solved = [None] * count
    for p in reversed(range(count)):
        running = rhs[p]
        for j in range(p + 1, count):
            running = running - gram[p][j] * solved[j]
        solved[p] = running * inverse[p]
    scale = sign[0] * solved[0]
    for k in range(1, count):
        scale = scale + sign[k] * solved[k]
    scale = 1.0 / scale
    leftover = [s * scale for s in solved]
    coefficients = [(1.0 - leftover[0]) * (1.0 / SHIFT)]
    for k in range(1, STEPS):
        coefficients.append(leftover[k] * (-1.0 / SHIFT) - coefficients[-1])
    return coefficients, leftover


def combine(plan, chunk, parts, v_ext, rims, *refs):
    basis, outs, buffers, sems = refs[:STEPS], refs[STEPS : STEPS + 2], refs[-3:-1], refs[-1]
    coefficients, leftover = weigh(parts[...])
    weights = coefficients + leftover
    own = plan.own()
    lane = lanes()

    def mix(refs, p, at):
        fields = [ref[p, at, :] for ref in refs]
        one, two = weights[0] * fields[0], weights[STEPS] * fields[0]
        for k in range(1, STEPS):
            one = one + weights[k] * fields[k]
            two = two + weights[STEPS + k] * fields[k]
        return one, two + weights[2 * STEPS] * fields[STEPS]

    copies = []
    for p in range(plan.nx):
        plane = own + p
        band = plane // plan.rim
        depth = plane - band * plan.rim
        low = 100 - BAND * band
        low = jnp.where(low < 0, low + 128, low)
        high = 116 - BAND * band
        for r in range(plan.ny // 8):
            at = pl.ds(TOP + 8 * r, 8)
            mains = mix((v_ext,) + tuple(basis), 1 + plane, at)
            edges = mix([rims.at[k] for k in range(STEPS + 1)], 1 + depth, at)
            for out, main, edge in zip(buffers, mains, edges):
                value = jnp.where(lane < STEPS, pltpu.roll(edge, low, 1), main)
                value = jnp.where(lane >= 128 - STEPS, pltpu.roll(edge, high, 1), value)
                out[p, pl.ds(8 * r, 8), :] = value
        if (p + 1) % chunk == 0:
            there = pl.ds(p + 1 - chunk, chunk)
            for f, (buffer, out) in enumerate(zip(buffers, outs)):
                sem = sems.at[f, p // chunk]
                copies.append(pltpu.make_async_copy(buffer.at[there], out.at[there], sem))
                copies[-1].start()
    for copy in copies:
        copy.wait()


def swaps(first, second, axis):
    count = lax.axis_size(axis)
    starts = (0, 1) if axis == "gy" else (1, 0)
    ones, twos = ([(i, i + 1) for i in range(s, count - 1, 2)] for s in starts)
    return tuple(
        lax.ppermute(value, axis, pairs + [(b, a) for a, b in pairs])
        for value, pairs in ((first, ones), (second, twos))
    )


def on_device(mesh, right_side, inv_density, active):
    nx, ny, nz = right_side.shape
    plan = Plan(mesh, nx, ny, nz)
    table = kept((plan.planes + 2, plan.tall, 128))
    face = kept((2, STEPS, ny, nz))
    inputs = [
        pltpu.with_memory_space_constraint(a, pltpu.HBM) for a in (right_side, inv_density, active)
    ]
    v_ext, w_ext, *faces = call(
        functools.partial(prepare, plan), [table, table] + [face] * plan.sides, "prepare"
    )(*inputs)
    if plan.sides == 1:
        halos = [lax.ppermute(faces[0], "gx", [(0, 1), (1, 0)])]
    else:
        steps = [(i, i + 1) for i in range(plan.gx - 1)]
        pairs = [steps, [(b, a) for a, b in steps]]
        halos = [lax.ppermute(f, "gx", p) for f, p in zip(faces, pairs)]
    strip = kept((2, plan.strip_rows(), 128))
    v_ext, w_ext, first, second = call(
        functools.partial(pack_rows, plan), [table, table, strip, strip], "rows", aliases={0: 0, 1: 1}
    )(*[resident(a) for a in (v_ext, w_ext, *halos)])
    first, second = swaps(first, second, "gy")
    rim = kept((plan.rim + 2, plan.tall, 128))
    packed, rim_v, rim_w, *fields = call(
        functools.partial(near, plan),
        [kept((2, plan.deep, plan.rows, 128)), rim, rim] + [table] * (4 + STEPS),
        "near",
        flops=1 << 24,
    )(resident(v_ext), resident(w_ext))
    column = kept((2, plan.deep, plan.half, 128))
    v_ext, w_ext, first, second = call(
        functools.partial(pack_lanes, plan),
        [table, table, column, column],
        "columns",
        aliases={0: 0, 1: 1},
    )(*[resident(a) for a in (v_ext, w_ext, first, second, packed)])
    first, second = swaps(first, second, "gz")
    v_ext, w_ext = resident(v_ext), resident(w_ext)
    devices = plan.gx * plan.gy * plan.gz
    sums = kept((2 * STEPS + 1, 8, 128))
    sums, rim_v, rim_w, *fields = call(
        functools.partial(inner, plan),
        [sums, rim, rim] + [table] * (4 + STEPS),
        "inner",
        aliases={i: i - 1 for i in range(2, 8 + STEPS)},
        flops=1 << 24,
    )(v_ext, w_ext, *[resident(a) for a in (rim_v, rim_w, *fields)])
    basis = fields[4:]
    rims, moments = call(
        functools.partial(outer, plan),
        [kept((STEPS + 1, plan.rim + 2, plan.tall, 128)), kept((devices, 1, 128))],
        "outer",
        scratch=[rim] * 5,
    )(*[resident(a) for a in (first, second, rim_v, rim_w, sums)])
    parts = lax.all_to_all(moments, AXES, 0, 0, tiled=True)
    chunk = 4
    shape = jax.ShapeDtypeStruct((nx, ny, nz), jnp.float32)
    operands = [parts, v_ext, rims] + basis
    out, residual = pl.pallas_call(
        functools.partial(combine, plan, chunk),
        out_shape=[shape, shape],
        in_specs=[vmem_spec()] * len(operands),
        out_specs=[pl.BlockSpec(memory_space=pl.ANY)] * 2,
        scratch_shapes=[kept((nx, ny, nz))] * 2 + [pltpu.SemaphoreType.DMA((2, nx // chunk))],
        compiler_params=pltpu.CompilerParams(vmem_limit_bytes=40 << 20),
        name="combine",
    )(*[resident(a) for a in operands])
    return out, residual


def solution(mesh):
    placed = P("gx", "gy", "gz")
    return jax.shard_map(
        functools.partial(on_device, mesh),
        mesh=mesh,
        in_specs=(placed,) * 3,
        out_specs=(placed, placed),
        check_vma=False,
    )
```

```python
import functools

import jax
import jax.numpy as jnp
from jax import lax
from jax.experimental import pallas as pl
from jax.experimental.pallas import tpu as pltpu
from jax.sharding import PartitionSpec as P

STEPS = 6
SHIFT = 7.0
GROUPS = 8
WIDE = 16
RIMS = 3
BAND = 40
EARLY = 3
QUAD = 4
TOP = 8
VMEM = pltpu.VMEM
AXES = ("gx", "gy", "gz")


def vmem_spec():
    return pl.BlockSpec(memory_space=VMEM)


def resident(array):
    return pltpu.with_memory_space_constraint(array, VMEM)


def call(body, outs, name, scratch=(), aliases=None, flops=0):
    return pl.pallas_call(
        body,
        out_shape=outs,
        out_specs=[vmem_spec() for _ in outs],
        scratch_shapes=list(scratch),
        input_output_aliases=aliases or {},
        compiler_params=pltpu.CompilerParams(vmem_limit_bytes=40 << 20),
        cost_estimate=pl.CostEstimate(flops=flops, bytes_accessed=1 << 20, transcendentals=0),
        name=name,
    )


def kept(shape):
    return pltpu.VMEM(shape, jnp.float32)


def lanes(shape=(8, 128)):
    return lax.broadcasted_iota(jnp.int32, shape, len(shape) - 1)


class Plan:
    def __init__(self, mesh, nx, ny, nz):
        self.gx, self.gy, self.gz = (mesh.shape[a] for a in AXES)
        self.nx, self.ny, self.nz = nx, ny, nz
        self.sides = min(self.gx - 1, 2)
        self.planes = nx + STEPS * self.sides
        self.deep = self.planes // GROUPS + 1
        self.rows = ny + 16
        self.half = self.rows // 2
        self.tall = self.rows + 16
        self.rim = self.planes // RIMS + 1

    def own(self):
        if self.sides == 1:
            return lax.axis_index("gx") * STEPS
        return STEPS if self.sides == 2 else 0

    def face_starts(self):
        if self.sides == 1:
            return [(1 - lax.axis_index("gx")) * (self.nx - STEPS)]
        return [self.nx - STEPS, 0]

    def halo_starts(self):
        if self.sides == 1:
            return [(1 - lax.axis_index("gx")) * self.nx]
        return [0, STEPS + self.nx] if self.sides == 2 else []

    def strips(self):
        parts = [(None, i, STEPS) for i in range(self.nx)]
        for side in range(self.sides):
            for distance in range(1, STEPS):
                toward, away = STEPS - distance, distance - 1
                if self.sides == 1:
                    index = lax.axis_index("gx")
                    plane = index * toward + (1 - index) * away
                else:
                    plane = away if side else toward
                parts.append((side, plane, STEPS - distance))
        return parts

    def strip_rows(self):
        return self.nx * STEPS + self.sides * STEPS * (STEPS - 1) // 2

    def span(self, level):
        if self.sides == 1:
            index = lax.axis_index("gx")
            return level * index, self.planes - level
        cut = level if self.sides == 2 else 0
        return cut, self.planes - 2 * cut


def prepare(plan, rs, inv, act, v_ext, w_ext, *edges):
    own, ny = 1 + plan.own(), plan.ny
    for ext in (v_ext, w_ext):
        ext[...] = jnp.zeros(ext.shape, jnp.float32)
    for i in range(plan.nx):
        liquid = act[i].astype(jnp.float32)
        v_ext[own + i, pl.ds(TOP, ny), :] = rs[i] * liquid
        w_ext[own + i, pl.ds(TOP, ny), :] = inv[i] * liquid * (2.0 / SHIFT)
    for start, edge in zip(plan.face_starts(), edges):
        for field, ext in enumerate((v_ext, w_ext)):
            for i in range(STEPS):
                p = own + start + i
                edge[field, i, pl.ds(0, 8), :] = ext[p, pl.ds(TOP, 8), :]
                edge[field, i, pl.ds(8, 8), :] = ext[p, pl.ds(TOP + ny - 8, 8), :]


def pack_rows(plan, v_ext, w_ext, *refs):
    edges, (first, second, *faces) = refs[: plan.sides], refs[plan.sides :]
    own, ny = 1 + plan.own(), plan.ny
    for start, face in zip(plan.face_starts(), faces):
        for field, ext in enumerate((v_ext, w_ext)):
            for i in range(STEPS):
                face[field, i] = ext[own + start + i, pl.ds(TOP, ny), :]
    even = lax.axis_index("gy") % 2 == 0
    for field, ext in enumerate((v_ext, w_ext)):
        offset = 0
        for side, plane, rows in plan.strips():
            if side is None:
                low = ext[own + plane, pl.ds(TOP, rows), :]
                high = ext[own + plane, pl.ds(TOP + ny - rows, rows), :]
            else:
                low = edges[side][field, plane, pl.ds(0, rows), :]
                high = edges[side][field, plane, pl.ds(16 - rows, rows), :]
            first[field, pl.ds(offset, rows), :] = jnp.where(even, high, low)
            second[field, pl.ds(offset, rows), :] = jnp.where(even, low, high)
            offset += rows


def column_block(plan, ext, i, r, group):
    block = jnp.zeros((8, 128), jnp.float32)
    for g in range(GROUPS):
        p = g * plan.deep + i
        if p < plan.planes:
            moved = pltpu.roll(ext[1 + p, pl.ds(8 * r, 8), :], WIDE * g + 8, 1)
            block = jnp.where(group == g, moved, block)
    return block


def rim_block(plan, ext, i, at, band, spot):
    block = jnp.zeros((8, 128), jnp.float32)
    for g in range(RIMS):
        p = g * plan.rim + i
        if p < plan.planes:
            value = ext[1 + p, at, :]
            high = pltpu.roll(value, BAND * g + 12, 1)
            low = pltpu.roll(value, (BAND * g + 28) % 128, 1)
            block = jnp.where((band == g) & (spot < 12), high, block)
            block = jnp.where((band == g) & (spot >= 28), low, block)
    return block


def near(plan, *refs):
    halos, (v_ext, w_ext, packed, rim_v, rim_w, *refs) = refs[2 : 2 + plan.sides], refs[2 + plan.sides :]
    tables, basis = refs[:4], refs[4:]
    planes = plan.planes
    inside = range(1, 1 + plan.ny // 8)
    for start, halo in zip(plan.halo_starts(), halos):
        for field, ext in enumerate((v_ext, w_ext)):
            for i in range(STEPS):
                ext[1 + start + i, pl.ds(TOP, plan.ny), :] = halo[field, i]
    for p in range(planes + 2):
        tables[1][p, pl.ds(TOP, 8), :] = jnp.zeros((8, 128), jnp.float32)
    face_tables(w_ext, tables, planes, planes // 2, inside, inside, inside)
    group = lanes() // WIDE
    band, spot = lanes() // BAND, lanes() % BAND
    for field, (ext, rim) in enumerate(((v_ext, rim_v), (w_ext, rim_w))):
        for r in inside:
            at = pl.ds(8 * r, 8)
            for i in range(plan.deep):
                packed[field, i, at, :] = column_block(plan, ext, i, r, group)
            for i in range(plan.rim):
                rim[1 + i, at, :] = rim_block(plan, ext, i, at, band, spot)
    for ref in basis:
        ref[0] = jnp.zeros(ref.shape[1:], jnp.float32)
        ref[planes + 1] = jnp.zeros(ref.shape[1:], jnp.float32)
    source = v_ext
    for level in range(1, EARLY + 1):
        sweep(plan, level, source, basis[level - 1], tables, [8 * r for r in inside])
        source = basis[level - 1]


def pack_lanes(plan, *refs):
    from_first, from_second, packed, v_ext, w_ext, first, second = refs[2:]
    ny = plan.ny
    even_y = lax.axis_index("gy") % 2 == 0
    even_z = lax.axis_index("gz") % 2 == 1
    lane = lanes()
    group = lane // WIDE
    right_half = (lane % WIDE) >= WIDE // 2
    starts = plan.halo_starts()
    last = plan.rows // 8 - 1
    for field, ext in enumerate((v_ext, w_ext)):
        offset = 0
        for side, plane, rows in plan.strips():
            at = 1 + plane + (plan.own() if side is None else starts[side])
            one = from_first[field, pl.ds(offset, rows), :]
            two = from_second[field, pl.ds(offset, rows), :]
            ext[at, pl.ds(TOP - rows, rows), :] = jnp.where(even_y, two, one)
            ext[at, pl.ds(TOP + ny, rows), :] = jnp.where(even_y, one, two)
            offset += rows
    for field, ext in enumerate((v_ext, w_ext)):
        for i in range(plan.deep):
            blocks = [packed[field, i, pl.ds(8 * r, 8), :] for r in range(1, last)]
            blocks = [column_block(plan, ext, i, 0, group)] + blocks
            blocks = blocks + [column_block(plan, ext, i, last, group)]
            for r in range(plan.half // 8):
                upper, lower = blocks[r], blocks[plan.half // 8 + r]
                to_right = jnp.where(right_half, pltpu.roll(lower, 8, 1), upper)
                to_left = jnp.where(right_half, lower, pltpu.roll(upper, 120, 1))
                first[field, i, pl.ds(8 * r, 8), :] = jnp.where(even_z, to_right, to_left)
                second[field, i, pl.ds(8 * r, 8), :] = jnp.where(even_z, to_left, to_right)


def coupling(one, two):
    total = jnp.maximum(one + two, 0.0625)
    inverse = pl.reciprocal(total, approx=True)
    inverse = inverse * (2.0 - total * inverse)
    return (one * two) * inverse


def face_tables(weight, tables, planes, unroll, across, along, diagonals):
    cx, cy, cz, dg = tables

    for r in across:
        at = pl.ds(8 * r, 8)
        cx[0, at, :] = coupling(weight[0, at, :], weight[1, at, :])

    def faces(trip, _):
        for u in range(unroll):
            p = 1 + unroll * trip + u
            for r in sorted({*across, *along}):
                at = pl.ds(8 * r, 8)
                here = weight[p, at, :]
                if r in across:
                    cx[p, at, :] = coupling(here, weight[p + 1, at, :])
                    cz[p, at, :] = coupling(here, pltpu.roll(here, 127, 1))
                if r in along:
                    below = weight[p, pl.ds(8 * r + 1, 8), :]
                    cy[p, pl.ds(8 * r + 8, 8), :] = coupling(here, below)
        return 0

    lax.fori_loop(0, planes // unroll, faces, 0)

    def diagonal(trip, _):
        for u in range(unroll):
            p = 1 + unroll * trip + u
            for r in diagonals:
                at = pl.ds(8 * r, 8)
                air = 0.5 * weight[p, at, :]
                total = jnp.full((8, 128), -1.0, jnp.float32)
                ahead = cz[p, at, :]
                for face in (
                    cx[p, at, :],
                    cx[p - 1, at, :],
                    cy[p, pl.ds(8 * r + 8, 8), :],
                    cy[p, pl.ds(8 * r + 7, 8), :],
                    ahead,
                    pltpu.roll(ahead, 1, 1),
                ):
                    total = total + jnp.where(face > 0.0, face, air)
                dg[p, at, :] = total
        return 0

    lax.fori_loop(0, planes // unroll, diagonal, 0)


def advance(source, target, tables, first, trips, unroll, starts):
    cx, cy, cz, dg = tables

    def body(trip, _):
        base = first + trip * unroll
        for u0, s in [(u0, s) for u0 in range(0, unroll, QUAD) for s in starts]:
            at = pl.ds(s, 8)
            top = min(u0 + QUAD, unroll)
            fields = {u: source[base + u, at, :] for u in range(u0, top + 2)}
            walls = {u: cx[base + u, at, :] for u in range(u0, top + 1)}
            for u in range(u0, top):
                p = base + u + 1
                here, ahead = fields[u + 1], cz[p, at, :]
                after = pltpu.roll(here, 127, 1)
                behind = pltpu.roll(ahead * here, 1, 1)
                total = walls[u + 1] * fields[u + 2] + walls[u] * fields[u]
                total = total + cy[p, pl.ds(s + 8, 8), :] * source[p, pl.ds(s + 1, 8), :]
                total = total + cy[p, pl.ds(s + 7, 8), :] * source[p, pl.ds(s - 1, 8), :]
                total = total + (ahead * after + behind)
                target[p, at, :] = dg[p, at, :] * here - total
        return 0

    if trips == 1:
        body(0, 0)
    else:
        lax.fori_loop(0, trips, body, 0)


def march(source, target, tables, first, trips, unroll, starts):
    cx, cy, cz, dg = tables
    row = lax.broadcasted_iota(jnp.int32, (8, 128), 0)
    top_row, end_row = row == 0, row == 7

    def body(trip, _):
        base = first + trip * unroll
        for u0 in range(0, unroll, QUAD):
            here = {u: None for u in range(u0, min(u0 + QUAD, unroll))}
            lifted, passed = {}, {}
            for s in starts:
                at, beyond = pl.ds(s, 8), pl.ds(s + 8, 8)
                for u in here:
                    p = base + u + 1
                    if s == starts[0]:
                        here[u] = source[p, at, :]
                        lifted[u] = pltpu.roll(here[u], 7, 0)
                        if s:
                            previous = cy[p, at, :] * source[p, pl.ds(s - 8, 8), :]
                            passed[u] = pltpu.roll(previous, 1, 0)
                fields = {u + 1: value for u, value in here.items()}
                fields[u0] = source[base + u0, at, :]
                final = max(here)
                fields[final + 2] = source[base + final + 2, at, :]
                walls = {u: cx[base + u, at, :] for u in range(u0, final + 2)}
                for u in here:
                    p = base + u + 1
                    value, ahead = here[u], cz[p, at, :]
                    wall = cy[p, beyond, :]
                    after = pltpu.roll(value, 127, 1)
                    behind = pltpu.roll(ahead * value, 1, 1)
                    sunk = pltpu.roll(wall * value, 1, 0)
                    upper = jnp.where(top_row, passed.get(u, sunk), sunk)
                    passed[u] = sunk
                    here[u] = source[p, beyond, :]
                    rising = pltpu.roll(here[u], 7, 0)
                    lower = jnp.where(end_row, rising, lifted[u])
                    lifted[u] = rising
                    total = walls[u + 1] * fields[u + 2] + walls[u] * fields[u]
                    total = total + (wall * lower + upper)
                    total = total + (ahead * after + behind)
                    target[p, at, :] = dg[p, at, :] * value - total
        return 0

    if trips == 1:
        body(0, 0)
    else:
        lax.fori_loop(0, trips, body, 0)


def sweep(plan, level, source, target, tables, starts):
    low, count = plan.span(level)
    half = -(-count // 2)
    low = jnp.minimum(low, plan.planes - 2 * half)
    march(source, target, tables, low, 2, half, starts)


def level_rows(plan, level):
    return range(0, plan.rows, 8) if level < STEPS else range(TOP, TOP + plan.ny, 8)


def products(fields, sums):
    for k in range(STEPS + 1):
        sums[2 * k] = sums[2 * k] + fields[k] * fields[k]
        if k < STEPS:
            sums[2 * k + 1] = sums[2 * k + 1] + fields[k] * fields[k + 1]
    return sums


def inner(plan, *refs):
    v_ext, w_ext = refs[:2]
    sums_ref, rim_v, rim_w, *refs = refs[8 + STEPS :]
    tables, basis = refs[:4], refs[4:]
    planes = plan.planes
    blank8 = jnp.zeros((8, 128), jnp.float32)
    last = plan.rows // 8 - 1
    halo = (0, last)
    face_tables(w_ext, tables, planes, planes // 2, halo, (0, last - 1, last), (0, 1, last - 1, last))
    source = v_ext
    for level in range(1, STEPS + 1):
        if level <= EARLY:
            low, count = plan.span(level)
            starts = [TOP - STEPS + level, TOP + plan.ny - 2 - level]
            advance(source, basis[level - 1], tables, low, 1, count, starts)
        else:
            sweep(plan, level, source, basis[level - 1], tables, level_rows(plan, level))
        source = basis[level - 1]

    own = 1 + plan.own()

    def gather(p, sums):
        sums = list(sums)
        for r in range(plan.ny // 8):
            at = pl.ds(TOP + 8 * r, 8)
            sums = products([ref[own + p, at, :] for ref in (v_ext,) + tuple(basis)], sums)
        return tuple(sums)

    sums = lax.fori_loop(0, plan.nx, gather, (blank8,) * (2 * STEPS + 1))
    lane = lanes()
    fresh = (lane >= STEPS) & (lane < 128 - STEPS)
    for j, part in enumerate(sums):
        sums_ref[j] = jnp.where(fresh, part, 0.0)

    band, spot = lane // BAND, lane % BAND
    for ext, rim in ((v_ext, rim_v), (w_ext, rim_w)):
        for r in halo:
            at = pl.ds(8 * r, 8)
            for i in range(plan.rim):
                rim[1 + i, at, :] = rim_block(plan, ext, i, at, band, spot)


def outer(plan, first, second, rim_v, rim_w, sums_ref, *refs):
    levels, moments, rim_s, *tables = refs
    rim_0, *basis = [levels.at[k] for k in range(STEPS + 1)]
    planes, deep, half, rim = plan.planes, plan.deep, plan.half, plan.rim
    even_z = lax.axis_index("gz") % 2 == 1
    lane = lanes()
    right_half = (lane % WIDE) >= WIDE // 2
    band, spot = lane // BAND, lane % BAND
    halo = (spot >= 12) & (spot < 28)
    blank8 = jnp.zeros((8, 128), jnp.float32)

    def wrap(ref, starts):
        for start in starts:
            at = pl.ds(start, 8)
            ref[0, at, :] = pltpu.roll(ref[rim, at, :], BAND, 1)
            ref[rim + 1, at, :] = pltpu.roll(ref[1, at, :], 128 - BAND, 1)

    for field, (own, full) in enumerate(((rim_v, rim_0), (rim_w, rim_s))):
        columns = [[None] * (2 * (half // 8)) for _ in range(deep)]
        for i in range(deep):
            for r in range(half // 8):
                one = first[field, i, pl.ds(8 * r, 8), :]
                two = second[field, i, pl.ds(8 * r, 8), :]
                left = jnp.where(even_z, two, one)
                right = jnp.where(even_z, one, two)
                columns[i][r] = jnp.where(right_half, pltpu.roll(left, 8, 1), right)
                columns[i][half // 8 + r] = jnp.where(right_half, left, pltpu.roll(right, 120, 1))
        for r in range(plan.rows // 8):
            at = pl.ds(8 * r, 8)
            for i in range(rim):
                block = own[1 + i, at, :]
                for g in range(RIMS):
                    p = g * rim + i
                    if p < planes:
                        turn = (BAND * g + 12 - WIDE * (p // deep)) % 128
                        moved = pltpu.roll(columns[p % deep][r], turn, 1)
                        block = jnp.where((band == g) & halo, moved, block)
                full[1 + i, at, :] = block
        for i in range(rim + 2):
            full[i, pl.ds(plan.rows, 16), :] = jnp.zeros((16, 128), jnp.float32)
        wrap(full, range(0, plan.rows, 8))

    every = range(plan.rows // 8)
    face_tables(rim_s, tables, rim, rim, every, every, every)
    source = rim_0
    for level in range(1, STEPS + 1):
        starts = level_rows(plan, level)
        target = basis[level - 1]
        march(source, target, tables, 0, 1, 1, starts)
        march(source, target, tables, rim - 1, 1, 1, starts)
        if level < STEPS:
            wrap(target, starts)
        march(source, target, tables, 1, 1, rim - 2, starts)
        source = target

    own = plan.own()
    fresh = ((spot >= 6) & (spot < 12)) | ((spot >= 28) & (spot < 34))
    sums = [sums_ref[j] for j in range(2 * STEPS + 1)]
    for i in range(rim):
        part = [blank8] * (2 * STEPS + 1)
        for r in range(plan.ny // 8):
            at = pl.ds(TOP + 8 * r, 8)
            part = products([ref[1 + i, at, :] for ref in (rim_0,) + tuple(basis)], part)
        plane = band * rim + i
        mine = fresh & (plane >= own) & (plane < own + plan.nx)
        sums = [a + jnp.where(mine, b, 0.0) for a, b in zip(sums, part)]
    row = lax.broadcasted_iota(jnp.int32, (16, 128), 0)
    stacked = jnp.zeros((16, 128), jnp.float32)
    for j, part in enumerate(sums):
        stacked = jnp.where(row == j, jnp.sum(part, axis=0, keepdims=True), stacked)
    stacked = jnp.sum(stacked, axis=1, keepdims=True)
    line = jnp.sum(jnp.where(lanes((16, 128)) == row, stacked, 0.0), axis=0, keepdims=True)
    for j in range(moments.shape[0]):
        moments[j] = line


def weigh(parts):
    lines = [parts[i] for i in range(parts.shape[0])]
    while len(lines) > 1:
        lines = [sum(lines[i + 1 : i + 2], lines[i]) for i in range(0, len(lines), 2)]
    line = jnp.broadcast_to(lines[0], (8, 128))
    moment = []
    for j in range(2 * STEPS + 1):
        picked = jnp.where(lanes() == j, line, 0.0)
        moment.append(jnp.broadcast_to(jnp.sum(picked, axis=1, keepdims=True), (8, 128)))
    count = STEPS + 1
    gram = [[moment[i + j] for j in range(count)] for i in range(count)]
    sign = [1.0 if k % 2 == 0 else -1.0 for k in range(count)]
    rhs = [jnp.full((8, 128), s, jnp.float32) for s in sign]
    inverse = []
    for p in range(count):
        inverse.append(1.0 / gram[p][p])
        for i in range(p + 1, count):
            factor = gram[p][i] * inverse[p]
            for j in range(i, count):
                gram[i][j] = gram[i][j] - factor * gram[p][j]
            rhs[i] = rhs[i] - factor * rhs[p]
    solved = [None] * count
    for p in reversed(range(count)):
        solved[p] = rhs[p] * inverse[p]
        for i in range(p):
            rhs[i] = rhs[i] - gram[i][p] * solved[p]
    scale = sign[0] * solved[0]
    for k in range(1, count):
        scale = scale + sign[k] * solved[k]
    scale = 1.0 / scale
    leftover = [s * scale for s in solved]
    coefficients = [(1.0 - leftover[0]) * (1.0 / SHIFT)]
    for k in range(1, STEPS):
        coefficients.append(leftover[k] * (-1.0 / SHIFT) - coefficients[-1])
    return coefficients, leftover


def combine(plan, chunk, parts, v_ext, rims, *refs):
    basis, outs, buffers, sems = refs[:STEPS], refs[STEPS : STEPS + 2], refs[-3:-1], refs[-1]
    coefficients, leftover = weigh(parts[...])
    weights = coefficients + leftover
    own = plan.own()
    lane = lanes()

    def mix(refs, p, at):
        fields = [ref[p, at, :] for ref in refs]
        one, two = weights[0] * fields[0], weights[STEPS] * fields[0]
        for k in range(1, STEPS):
            one = one + weights[k] * fields[k]
            two = two + weights[STEPS + k] * fields[k]
        return one, two + weights[2 * STEPS] * fields[STEPS]

    copies = []
    for p in range(plan.nx):
        plane = own + p
        band = plane // plan.rim
        depth = plane - band * plan.rim
        low = 100 - BAND * band
        low = jnp.where(low < 0, low + 128, low)
        high = 116 - BAND * band
        for r in range(plan.ny // 8):
            at = pl.ds(TOP + 8 * r, 8)
            mains = mix((v_ext,) + tuple(basis), 1 + plane, at)
            edges = mix([rims.at[k] for k in range(STEPS + 1)], 1 + depth, at)
            for out, main, edge in zip(buffers, mains, edges):
                value = jnp.where(lane < STEPS, pltpu.roll(edge, low, 1), main)
                value = jnp.where(lane >= 128 - STEPS, pltpu.roll(edge, high, 1), value)
                out[p, pl.ds(8 * r, 8), :] = value
        if (p + 1) % chunk == 0:
            there = pl.ds(p + 1 - chunk, chunk)
            for f, (buffer, out) in enumerate(zip(buffers, outs)):
                sem = sems.at[f, p // chunk]
                copies.append(pltpu.make_async_copy(buffer.at[there], out.at[there], sem))
                copies[-1].start()
    for copy in copies:
        copy.wait()


def across(plan, values):
    if plan.sides == 1:
        return [lax.ppermute(values[0], "gx", [(0, 1), (1, 0)])]
    steps = [(i, i + 1) for i in range(plan.gx - 1)]
    pairs = [steps, [(b, a) for a, b in steps]]
    return [lax.ppermute(value, "gx", p) for value, p in zip(values, pairs)]


def swaps(first, second, axis):
    count = lax.axis_size(axis)
    starts = (0, 1) if axis == "gy" else (1, 0)
    ones, twos = ([(i, i + 1) for i in range(s, count - 1, 2)] for s in starts)
    return tuple(
        lax.ppermute(value, axis, pairs + [(b, a) for a, b in pairs])
        for value, pairs in ((first, ones), (second, twos))
    )


def on_device(mesh, right_side, inv_density, active):
    nx, ny, nz = right_side.shape
    plan = Plan(mesh, nx, ny, nz)
    table = kept((plan.planes + 2, plan.tall, 128))
    face = kept((2, STEPS, ny, nz))
    inputs = [
        pltpu.with_memory_space_constraint(a, pltpu.HBM) for a in (right_side, inv_density, active)
    ]
    edge = kept((2, STEPS, 16, 128))
    v_ext, w_ext, *edges = call(
        functools.partial(prepare, plan), [table, table] + [edge] * plan.sides, "prepare"
    )(*inputs)
    edges = across(plan, edges)
    strip = kept((2, plan.strip_rows(), 128))
    first, second, *faces = call(
        functools.partial(pack_rows, plan), [strip, strip] + [face] * plan.sides, "rows"
    )(*[resident(a) for a in (v_ext, w_ext, *edges)])
    halos = across(plan, faces)
    first, second = swaps(first, second, "gy")
    rim = kept((plan.rim + 2, plan.tall, 128))
    v_ext, w_ext, packed, rim_v, rim_w, *fields = call(
        functools.partial(near, plan),
        [table, table, kept((2, plan.deep, plan.rows, 128)), rim, rim] + [table] * (4 + STEPS),
        "near",
        aliases={0: 0, 1: 1},
        flops=1 << 24,
    )(*[resident(a) for a in (v_ext, w_ext, *halos)])
    column = kept((2, plan.deep, plan.half, 128))
    v_ext, w_ext, first, second = call(
        functools.partial(pack_lanes, plan),
        [table, table, column, column],
        "columns",
        aliases={0: 0, 1: 1},
    )(*[resident(a) for a in (v_ext, w_ext, first, second, packed)])
    first, second = swaps(first, second, "gz")
    v_ext, w_ext = resident(v_ext), resident(w_ext)
    devices = plan.gx * plan.gy * plan.gz
    sums = kept((2 * STEPS + 1, 8, 128))
    sums, rim_v, rim_w, *fields = call(
        functools.partial(inner, plan),
        [sums, rim, rim] + [table] * (4 + STEPS),
        "inner",
        aliases={i: i - 1 for i in range(2, 8 + STEPS)},
        flops=1 << 24,
    )(v_ext, w_ext, *[resident(a) for a in (rim_v, rim_w, *fields)])
    basis = fields[4:]
    rims, moments = call(
        functools.partial(outer, plan),
        [kept((STEPS + 1, plan.rim + 2, plan.tall, 128)), kept((devices, 1, 128))],
        "outer",
        scratch=[rim] * 5,
    )(*[resident(a) for a in (first, second, rim_v, rim_w, sums)])
    parts = lax.all_to_all(moments, AXES, 0, 0, tiled=True)
    chunk = 4
    shape = jax.ShapeDtypeStruct((nx, ny, nz), jnp.float32)
    operands = [parts, v_ext, rims] + basis
    out, residual = pl.pallas_call(
        functools.partial(combine, plan, chunk),
        out_shape=[shape, shape],
        in_specs=[vmem_spec()] * len(operands),
        out_specs=[pl.BlockSpec(memory_space=pl.ANY)] * 2,
        scratch_shapes=[kept((nx, ny, nz))] * 2 + [pltpu.SemaphoreType.DMA((2, nx // chunk))],
        compiler_params=pltpu.CompilerParams(vmem_limit_bytes=40 << 20),
        name="combine",
    )(*[resident(a) for a in operands])
    return out, residual


def solution(mesh):
    placed = P("gx", "gy", "gz")
    return jax.shard_map(
        functools.partial(on_device, mesh),
        mesh=mesh,
        in_specs=(placed,) * 3,
        out_specs=(placed, placed),
        check_vma=False,
    )
```

```python
import functools

import jax
import jax.numpy as jnp
from jax import lax
from jax.experimental import pallas as pl
from jax.experimental.pallas import tpu as pltpu
from jax.sharding import PartitionSpec as P

STEPS = 6
SHIFT = 7.0
GROUPS = 8
WIDE = 16
RIMS = 3
BAND = 40
EARLY = 3
QUAD = 4
TOP = 8
VMEM = pltpu.VMEM
AXES = ("gx", "gy", "gz")


def vmem_spec():
    return pl.BlockSpec(memory_space=VMEM)


def resident(array):
    return pltpu.with_memory_space_constraint(array, VMEM)


def call(body, outs, name, scratch=(), aliases=None, flops=0):
    return pl.pallas_call(
        body,
        out_shape=outs,
        out_specs=[vmem_spec() for _ in outs],
        scratch_shapes=list(scratch),
        input_output_aliases=aliases or {},
        compiler_params=pltpu.CompilerParams(vmem_limit_bytes=40 << 20),
        cost_estimate=pl.CostEstimate(flops=flops, bytes_accessed=1 << 20, transcendentals=0),
        name=name,
    )


def kept(shape):
    return pltpu.VMEM(shape, jnp.float32)


def lanes(shape=(8, 128)):
    return lax.broadcasted_iota(jnp.int32, shape, len(shape) - 1)


class Plan:
    def __init__(self, mesh, nx, ny, nz):
        self.gx, self.gy, self.gz = (mesh.shape[a] for a in AXES)
        self.nx, self.ny, self.nz = nx, ny, nz
        self.sides = min(self.gx - 1, 2)
        self.planes = nx + STEPS * self.sides
        self.deep = self.planes // GROUPS + 1
        self.rows = ny + 16
        self.half = self.rows // 2
        self.tall = self.rows + 16
        self.rim = self.planes // RIMS + 1

    def own(self):
        if self.sides == 1:
            return lax.axis_index("gx") * STEPS
        return STEPS if self.sides == 2 else 0

    def face_starts(self):
        if self.sides == 1:
            return [(1 - lax.axis_index("gx")) * (self.nx - STEPS)]
        return [self.nx - STEPS, 0]

    def halo_starts(self):
        if self.sides == 1:
            return [(1 - lax.axis_index("gx")) * self.nx]
        return [0, STEPS + self.nx] if self.sides == 2 else []

    def strips(self):
        parts = [(None, i, STEPS) for i in range(self.nx)]
        for side in range(self.sides):
            for distance in range(1, STEPS):
                toward, away = STEPS - distance, distance - 1
                if self.sides == 1:
                    index = lax.axis_index("gx")
                    plane = index * toward + (1 - index) * away
                else:
                    plane = away if side else toward
                parts.append((side, plane, STEPS - distance))
        return parts

    def strip_rows(self):
        return self.nx * STEPS + self.sides * STEPS * (STEPS - 1) // 2

    def span(self, level):
        if self.sides == 1:
            index = lax.axis_index("gx")
            return level * index, self.planes - level
        cut = level if self.sides == 2 else 0
        return cut, self.planes - 2 * cut


def prepare(plan, rs, inv, act, v_ext, w_ext, *edges):
    own, ny = 1 + plan.own(), plan.ny
    for ext in (v_ext, w_ext):
        ext[...] = jnp.zeros(ext.shape, jnp.float32)
    for i in range(plan.nx):
        liquid = act[i].astype(jnp.float32)
        v_ext[own + i, pl.ds(TOP, ny), :] = rs[i] * liquid
        w_ext[own + i, pl.ds(TOP, ny), :] = inv[i] * liquid * (2.0 / SHIFT)
    for start, edge in zip(plan.face_starts(), edges):
        for field, ext in enumerate((v_ext, w_ext)):
            for i in range(STEPS):
                p = own + start + i
                edge[field, i, pl.ds(0, 8), :] = ext[p, pl.ds(TOP, 8), :]
                edge[field, i, pl.ds(8, 8), :] = ext[p, pl.ds(TOP + ny - 8, 8), :]


def pack_rows(plan, v_ext, w_ext, *refs):
    edges, (first, second, *faces) = refs[: plan.sides], refs[plan.sides :]
    own, ny = 1 + plan.own(), plan.ny
    for start, face in zip(plan.face_starts(), faces):
        for field, ext in enumerate((v_ext, w_ext)):
            for i in range(STEPS):
                face[field, i] = ext[own + start + i, pl.ds(TOP, ny), :]
    even = lax.axis_index("gy") % 2 == 0
    for field, ext in enumerate((v_ext, w_ext)):
        offset = 0
        for side, plane, rows in plan.strips():
            if side is None:
                low = ext[own + plane, pl.ds(TOP, rows), :]
                high = ext[own + plane, pl.ds(TOP + ny - rows, rows), :]
            else:
                low = edges[side][field, plane, pl.ds(0, rows), :]
                high = edges[side][field, plane, pl.ds(16 - rows, rows), :]
            first[field, pl.ds(offset, rows), :] = jnp.where(even, high, low)
            second[field, pl.ds(offset, rows), :] = jnp.where(even, low, high)
            offset += rows


def column_block(plan, ext, i, r, group):
    block = jnp.zeros((8, 128), jnp.float32)
    for g in range(GROUPS):
        p = g * plan.deep + i
        if p < plan.planes:
            moved = pltpu.roll(ext[1 + p, pl.ds(8 * r, 8), :], WIDE * g + 8, 1)
            block = jnp.where(group == g, moved, block)
    return block


def rim_block(plan, ext, i, at, band, spot):
    block = jnp.zeros((8, 128), jnp.float32)
    for g in range(RIMS):
        p = g * plan.rim + i
        if p < plan.planes:
            value = ext[1 + p, at, :]
            high = pltpu.roll(value, BAND * g + 12, 1)
            low = pltpu.roll(value, (BAND * g + 28) % 128, 1)
            block = jnp.where((band == g) & (spot < 12), high, block)
            block = jnp.where((band == g) & (spot >= 28), low, block)
    return block


def near(plan, *refs):
    halos, (v_ext, w_ext, packed, rim_v, rim_w, *refs) = refs[2 : 2 + plan.sides], refs[2 + plan.sides :]
    tables, basis = refs[:4], refs[4:]
    planes = plan.planes
    inside = range(1, 1 + plan.ny // 8)
    for start, halo in zip(plan.halo_starts(), halos):
        for field, ext in enumerate((v_ext, w_ext)):
            for i in range(STEPS):
                ext[1 + start + i, pl.ds(TOP, plan.ny), :] = halo[field, i]
    for p in range(planes + 2):
        tables[1][p, pl.ds(TOP, 8), :] = jnp.zeros((8, 128), jnp.float32)
    face_tables(w_ext, tables, planes, planes // 2, inside, inside, inside)
    group = lanes() // WIDE
    band, spot = lanes() // BAND, lanes() % BAND
    for field, (ext, rim) in enumerate(((v_ext, rim_v), (w_ext, rim_w))):
        for r in inside:
            at = pl.ds(8 * r, 8)
            for i in range(plan.deep):
                packed[field, i, at, :] = column_block(plan, ext, i, r, group)
            for i in range(plan.rim):
                rim[1 + i, at, :] = rim_block(plan, ext, i, at, band, spot)
    for ref in basis:
        ref[0] = jnp.zeros(ref.shape[1:], jnp.float32)
        ref[planes + 1] = jnp.zeros(ref.shape[1:], jnp.float32)
    source = v_ext
    for level in range(1, EARLY + 1):
        sweep(plan, level, source, basis[level - 1], tables, [8 * r for r in inside])
        source = basis[level - 1]


def pack_lanes(plan, *refs):
    from_first, from_second, packed, v_ext, w_ext, first, second = refs[2:]
    ny = plan.ny
    even_y = lax.axis_index("gy") % 2 == 0
    even_z = lax.axis_index("gz") % 2 == 1
    lane = lanes()
    group = lane // WIDE
    right_half = (lane % WIDE) >= WIDE // 2
    starts = plan.halo_starts()
    last = plan.rows // 8 - 1
    for field, ext in enumerate((v_ext, w_ext)):
        offset = 0
        for side, plane, rows in plan.strips():
            at = 1 + plane + (plan.own() if side is None else starts[side])
            one = from_first[field, pl.ds(offset, rows), :]
            two = from_second[field, pl.ds(offset, rows), :]
            ext[at, pl.ds(TOP - rows, rows), :] = jnp.where(even_y, two, one)
            ext[at, pl.ds(TOP + ny, rows), :] = jnp.where(even_y, one, two)
            offset += rows
    for field, ext in enumerate((v_ext, w_ext)):
        for i in range(plan.deep):
            blocks = [packed[field, i, pl.ds(8 * r, 8), :] for r in range(1, last)]
            blocks = [column_block(plan, ext, i, 0, group)] + blocks
            blocks = blocks + [column_block(plan, ext, i, last, group)]
            for r in range(plan.half // 8):
                upper, lower = blocks[r], blocks[plan.half // 8 + r]
                to_right = jnp.where(right_half, pltpu.roll(lower, 8, 1), upper)
                to_left = jnp.where(right_half, lower, pltpu.roll(upper, 120, 1))
                first[field, i, pl.ds(8 * r, 8), :] = jnp.where(even_z, to_right, to_left)
                second[field, i, pl.ds(8 * r, 8), :] = jnp.where(even_z, to_left, to_right)


def coupling(one, two):
    total = jnp.maximum(one + two, 0.0625)
    inverse = pl.reciprocal(total, approx=True)
    inverse = inverse * (2.0 - total * inverse)
    return (one * two) * inverse


def face_tables(weight, tables, planes, unroll, across, along, diagonals):
    cx, cy, cz, dg = tables

    for r in across:
        at = pl.ds(8 * r, 8)
        cx[0, at, :] = coupling(weight[0, at, :], weight[1, at, :])

    def faces(trip, _):
        for u in range(unroll):
            p = 1 + unroll * trip + u
            for r in sorted({*across, *along}):
                at = pl.ds(8 * r, 8)
                here = weight[p, at, :]
                if r in across:
                    cx[p, at, :] = coupling(here, weight[p + 1, at, :])
                    cz[p, at, :] = coupling(here, pltpu.roll(here, 127, 1))
                if r in along:
                    below = weight[p, pl.ds(8 * r + 1, 8), :]
                    cy[p, pl.ds(8 * r + 8, 8), :] = coupling(here, below)
        return 0

    lax.fori_loop(0, planes // unroll, faces, 0)

    def diagonal(trip, _):
        for u in range(unroll):
            p = 1 + unroll * trip + u
            for r in diagonals:
                at = pl.ds(8 * r, 8)
                air = 0.5 * weight[p, at, :]
                total = jnp.full((8, 128), -1.0, jnp.float32)
                ahead = cz[p, at, :]
                for face in (
                    cx[p, at, :],
                    cx[p - 1, at, :],
                    cy[p, pl.ds(8 * r + 8, 8), :],
                    cy[p, pl.ds(8 * r + 7, 8), :],
                    ahead,
                    pltpu.roll(ahead, 1, 1),
                ):
                    total = total + jnp.where(face > 0.0, face, air)
                dg[p, at, :] = total
        return 0

    lax.fori_loop(0, planes // unroll, diagonal, 0)


def advance(source, target, tables, first, trips, unroll, starts):
    cx, cy, cz, dg = tables

    def body(trip, _):
        base = first + trip * unroll
        for u0, s in [(u0, s) for u0 in range(0, unroll, QUAD) for s in starts]:
            at = pl.ds(s, 8)
            top = min(u0 + QUAD, unroll)
            fields = {u: source[base + u, at, :] for u in range(u0, top + 2)}
            walls = {u: cx[base + u, at, :] for u in range(u0, top + 1)}
            for u in range(u0, top):
                p = base + u + 1
                here, ahead = fields[u + 1], cz[p, at, :]
                after = pltpu.roll(here, 127, 1)
                behind = pltpu.roll(ahead * here, 1, 1)
                total = walls[u + 1] * fields[u + 2] + walls[u] * fields[u]
                total = total + cy[p, pl.ds(s + 8, 8), :] * source[p, pl.ds(s + 1, 8), :]
                total = total + cy[p, pl.ds(s + 7, 8), :] * source[p, pl.ds(s - 1, 8), :]
                total = total + (ahead * after + behind)
                target[p, at, :] = dg[p, at, :] * here - total
        return 0

    if trips == 1:
        body(0, 0)
    else:
        lax.fori_loop(0, trips, body, 0)


def march(source, target, tables, first, trips, unroll, starts):
    cx, cy, cz, dg = tables
    row = lax.broadcasted_iota(jnp.int32, (8, 128), 0)
    top_row, end_row = row == 0, row == 7

    def body(trip, _):
        base = first + trip * unroll
        for u0 in range(0, unroll, QUAD):
            here = {u: None for u in range(u0, min(u0 + QUAD, unroll))}
            lifted, passed = {}, {}
            for s in starts:
                at, beyond = pl.ds(s, 8), pl.ds(s + 8, 8)
                for u in here:
                    p = base + u + 1
                    if s == starts[0]:
                        here[u] = source[p, at, :]
                        lifted[u] = pltpu.roll(here[u], 7, 0)
                        if s:
                            previous = cy[p, at, :] * source[p, pl.ds(s - 8, 8), :]
                            passed[u] = pltpu.roll(previous, 1, 0)
                fields = {u + 1: value for u, value in here.items()}
                fields[u0] = source[base + u0, at, :]
                final = max(here)
                fields[final + 2] = source[base + final + 2, at, :]
                walls = {u: cx[base + u, at, :] for u in range(u0, final + 2)}
                for u in here:
                    p = base + u + 1
                    value, ahead = here[u], cz[p, at, :]
                    wall = cy[p, beyond, :]
                    after = pltpu.roll(value, 127, 1)
                    behind = pltpu.roll(ahead * value, 1, 1)
                    sunk = pltpu.roll(wall * value, 1, 0)
                    upper = jnp.where(top_row, passed.get(u, sunk), sunk)
                    passed[u] = sunk
                    here[u] = source[p, beyond, :]
                    rising = pltpu.roll(here[u], 7, 0)
                    lower = jnp.where(end_row, rising, lifted[u])
                    lifted[u] = rising
                    total = walls[u + 1] * fields[u + 2] + walls[u] * fields[u]
                    total = total + (wall * lower + upper)
                    total = total + (ahead * after + behind)
                    target[p, at, :] = dg[p, at, :] * value - total
        return 0

    if trips == 1:
        body(0, 0)
    else:
        lax.fori_loop(0, trips, body, 0)


def sweep(plan, level, source, target, tables, starts):
    low, count = plan.span(level)
    half = -(-count // 2)
    low = jnp.minimum(low, plan.planes - 2 * half)
    move = advance if starts[0] else march
    move(source, target, tables, low, 2, half, starts)


def level_rows(plan, level):
    return range(0, plan.rows, 8) if level < STEPS else range(TOP, TOP + plan.ny, 8)


def products(fields, sums):
    for k in range(STEPS + 1):
        sums[2 * k] = sums[2 * k] + fields[k] * fields[k]
        if k < STEPS:
            sums[2 * k + 1] = sums[2 * k + 1] + fields[k] * fields[k + 1]
    return sums


def inner(plan, *refs):
    v_ext, w_ext = refs[:2]
    sums_ref, rim_v, rim_w, *refs = refs[8 + STEPS :]
    tables, basis = refs[:4], refs[4:]
    planes = plan.planes
    blank8 = jnp.zeros((8, 128), jnp.float32)
    last = plan.rows // 8 - 1
    halo = (0, last)
    face_tables(w_ext, tables, planes, planes // 2, halo, (0, last - 1, last), (0, 1, last - 1, last))
    source = v_ext
    for level in range(1, STEPS + 1):
        if level <= EARLY:
            low, count = plan.span(level)
            starts = [TOP - STEPS + level, TOP + plan.ny - 2 - level]
            advance(source, basis[level - 1], tables, low, 1, count, starts)
        else:
            sweep(plan, level, source, basis[level - 1], tables, level_rows(plan, level))
        source = basis[level - 1]

    own = 1 + plan.own()

    def gather(p, sums):
        sums = list(sums)
        for r in range(plan.ny // 8):
            at = pl.ds(TOP + 8 * r, 8)
            sums = products([ref[own + p, at, :] for ref in (v_ext,) + tuple(basis)], sums)
        return tuple(sums)

    sums = lax.fori_loop(0, plan.nx, gather, (blank8,) * (2 * STEPS + 1))
    lane = lanes()
    fresh = (lane >= STEPS) & (lane < 128 - STEPS)
    for j, part in enumerate(sums):
        sums_ref[j] = jnp.where(fresh, part, 0.0)

    band, spot = lane // BAND, lane % BAND
    for ext, rim in ((v_ext, rim_v), (w_ext, rim_w)):
        for r in halo:
            at = pl.ds(8 * r, 8)
            for i in range(plan.rim):
                rim[1 + i, at, :] = rim_block(plan, ext, i, at, band, spot)


def outer(plan, first, second, rim_v, rim_w, sums_ref, *refs):
    levels, moments, rim_s, *tables = refs
    rim_0, *basis = [levels.at[k] for k in range(STEPS + 1)]
    planes, deep, half, rim = plan.planes, plan.deep, plan.half, plan.rim
    even_z = lax.axis_index("gz") % 2 == 1
    lane = lanes()
    right_half = (lane % WIDE) >= WIDE // 2
    band, spot = lane // BAND, lane % BAND
    halo = (spot >= 12) & (spot < 28)
    blank8 = jnp.zeros((8, 128), jnp.float32)

    def wrap(ref, starts):
        for start in starts:
            at = pl.ds(start, 8)
            ref[0, at, :] = pltpu.roll(ref[rim, at, :], BAND, 1)
            ref[rim + 1, at, :] = pltpu.roll(ref[1, at, :], 128 - BAND, 1)

    for field, (own, full) in enumerate(((rim_v, rim_0), (rim_w, rim_s))):
        columns = [[None] * (2 * (half // 8)) for _ in range(deep)]
        for i in range(deep):
            for r in range(half // 8):
                one = first[field, i, pl.ds(8 * r, 8), :]
                two = second[field, i, pl.ds(8 * r, 8), :]
                left = jnp.where(even_z, two, one)
                right = jnp.where(even_z, one, two)
                columns[i][r] = jnp.where(right_half, pltpu.roll(left, 8, 1), right)
                columns[i][half // 8 + r] = jnp.where(right_half, left, pltpu.roll(right, 120, 1))
        for r in range(plan.rows // 8):
            at = pl.ds(8 * r, 8)
            for i in range(rim):
                block = own[1 + i, at, :]
                for g in range(RIMS):
                    p = g * rim + i
                    if p < planes:
                        turn = (BAND * g + 12 - WIDE * (p // deep)) % 128
                        moved = pltpu.roll(columns[p % deep][r], turn, 1)
                        block = jnp.where((band == g) & halo, moved, block)
                full[1 + i, at, :] = block
        for i in range(rim + 2):
            full[i, pl.ds(plan.rows, 16), :] = jnp.zeros((16, 128), jnp.float32)
        wrap(full, range(0, plan.rows, 8))

    every = range(plan.rows // 8)
    face_tables(rim_s, tables, rim, rim, every, every, every)
    source = rim_0
    for level in range(1, STEPS + 1):
        starts = level_rows(plan, level)
        target = basis[level - 1]
        march(source, target, tables, 0, 1, 1, starts)
        march(source, target, tables, rim - 1, 1, 1, starts)
        if level < STEPS:
            wrap(target, starts)
        march(source, target, tables, 1, 1, rim - 2, starts)
        source = target

    own = plan.own()
    fresh = ((spot >= 6) & (spot < 12)) | ((spot >= 28) & (spot < 34))
    sums = [sums_ref[j] for j in range(2 * STEPS + 1)]
    for i in range(rim):
        part = [blank8] * (2 * STEPS + 1)
        for r in range(plan.ny // 8):
            at = pl.ds(TOP + 8 * r, 8)
            part = products([ref[1 + i, at, :] for ref in (rim_0,) + tuple(basis)], part)
        plane = band * rim + i
        mine = fresh & (plane >= own) & (plane < own + plan.nx)
        sums = [a + jnp.where(mine, b, 0.0) for a, b in zip(sums, part)]
    row = lax.broadcasted_iota(jnp.int32, (16, 128), 0)
    stacked = jnp.zeros((16, 128), jnp.float32)
    for j, part in enumerate(sums):
        stacked = jnp.where(row == j, jnp.sum(part, axis=0, keepdims=True), stacked)
    stacked = jnp.sum(stacked, axis=1, keepdims=True)
    line = jnp.sum(jnp.where(lanes((16, 128)) == row, stacked, 0.0), axis=0, keepdims=True)
    for j in range(moments.shape[0]):
        moments[j] = line


def weigh(parts):
    lines = [parts[i] for i in range(parts.shape[0])]
    while len(lines) > 1:
        lines = [sum(lines[i + 1 : i + 2], lines[i]) for i in range(0, len(lines), 2)]
    line = jnp.broadcast_to(lines[0], (8, 128))
    moment = []
    for j in range(2 * STEPS + 1):
        picked = jnp.where(lanes() == j, line, 0.0)
        moment.append(jnp.broadcast_to(jnp.sum(picked, axis=1, keepdims=True), (8, 128)))
    count = STEPS + 1
    gram = [[moment[i + j] for j in range(count)] for i in range(count)]
    sign = [1.0 if k % 2 == 0 else -1.0 for k in range(count)]
    rhs = [jnp.full((8, 128), s, jnp.float32) for s in sign]
    inverse = []
    for p in range(count):
        inverse.append(1.0 / gram[p][p])
        for i in range(p + 1, count):
            factor = gram[p][i] * inverse[p]
            for j in range(i, count):
                gram[i][j] = gram[i][j] - factor * gram[p][j]
            rhs[i] = rhs[i] - factor * rhs[p]
    solved = [None] * count
    for p in reversed(range(count)):
        solved[p] = rhs[p] * inverse[p]
        for i in range(p):
            rhs[i] = rhs[i] - gram[i][p] * solved[p]
    scale = sign[0] * solved[0]
    for k in range(1, count):
        scale = scale + sign[k] * solved[k]
    scale = 1.0 / scale
    leftover = [s * scale for s in solved]
    coefficients = [(1.0 - leftover[0]) * (1.0 / SHIFT)]
    for k in range(1, STEPS):
        coefficients.append(leftover[k] * (-1.0 / SHIFT) - coefficients[-1])
    return coefficients, leftover


def combine(plan, chunk, parts, v_ext, rims, *refs):
    basis, outs, buffers, sems = refs[:STEPS], refs[STEPS : STEPS + 2], refs[-3:-1], refs[-1]
    coefficients, leftover = weigh(parts[...])
    weights = coefficients + leftover
    own = plan.own()
    lane = lanes()

    def mix(refs, p, at):
        fields = [ref[p, at, :] for ref in refs]
        one, two = weights[0] * fields[0], weights[STEPS] * fields[0]
        for k in range(1, STEPS):
            one = one + weights[k] * fields[k]
            two = two + weights[STEPS + k] * fields[k]
        return one, two + weights[2 * STEPS] * fields[STEPS]

    copies = []
    for p in range(plan.nx):
        plane = own + p
        band = plane // plan.rim
        depth = plane - band * plan.rim
        low = 100 - BAND * band
        low = jnp.where(low < 0, low + 128, low)
        high = 116 - BAND * band
        for r in range(plan.ny // 8):
            at = pl.ds(TOP + 8 * r, 8)
            mains = mix((v_ext,) + tuple(basis), 1 + plane, at)
            edges = mix([rims.at[k] for k in range(STEPS + 1)], 1 + depth, at)
            for out, main, edge in zip(buffers, mains, edges):
                value = jnp.where(lane < STEPS, pltpu.roll(edge, low, 1), main)
                value = jnp.where(lane >= 128 - STEPS, pltpu.roll(edge, high, 1), value)
                out[p, pl.ds(8 * r, 8), :] = value
        if (p + 1) % chunk == 0:
            there = pl.ds(p + 1 - chunk, chunk)
            for f, (buffer, out) in enumerate(zip(buffers, outs)):
                sem = sems.at[f, p // chunk]
                copies.append(pltpu.make_async_copy(buffer.at[there], out.at[there], sem))
                copies[-1].start()
    for copy in copies:
        copy.wait()


def across(plan, values):
    if plan.sides == 1:
        return [lax.ppermute(values[0], "gx", [(0, 1), (1, 0)])]
    steps = [(i, i + 1) for i in range(plan.gx - 1)]
    pairs = [steps, [(b, a) for a, b in steps]]
    return [lax.ppermute(value, "gx", p) for value, p in zip(values, pairs)]


def swaps(first, second, axis):
    count = lax.axis_size(axis)
    starts = (0, 1) if axis == "gy" else (1, 0)
    ones, twos = ([(i, i + 1) for i in range(s, count - 1, 2)] for s in starts)
    return tuple(
        lax.ppermute(value, axis, pairs + [(b, a) for a, b in pairs])
        for value, pairs in ((first, ones), (second, twos))
    )


def on_device(mesh, right_side, inv_density, active):
    nx, ny, nz = right_side.shape
    plan = Plan(mesh, nx, ny, nz)
    table = kept((plan.planes + 2, plan.tall, 128))
    face = kept((2, STEPS, ny, nz))
    inputs = [
        pltpu.with_memory_space_constraint(a, pltpu.HBM) for a in (right_side, inv_density, active)
    ]
    edge = kept((2, STEPS, 16, 128))
    v_ext, w_ext, *edges = call(
        functools.partial(prepare, plan), [table, table] + [edge] * plan.sides, "prepare"
    )(*inputs)
    edges = across(plan, edges)
    strip = kept((2, plan.strip_rows(), 128))
    first, second, *faces = call(
        functools.partial(pack_rows, plan), [strip, strip] + [face] * plan.sides, "rows"
    )(*[resident(a) for a in (v_ext, w_ext, *edges)])
    halos = across(plan, faces)
    first, second = swaps(first, second, "gy")
    rim = kept((plan.rim + 2, plan.tall, 128))
    v_ext, w_ext, packed, rim_v, rim_w, *fields = call(
        functools.partial(near, plan),
        [table, table, kept((2, plan.deep, plan.rows, 128)), rim, rim] + [table] * (4 + STEPS),
        "near",
        aliases={0: 0, 1: 1},
        flops=1 << 24,
    )(*[resident(a) for a in (v_ext, w_ext, *halos)])
    column = kept((2, plan.deep, plan.half, 128))
    v_ext, w_ext, first, second = call(
        functools.partial(pack_lanes, plan),
        [table, table, column, column],
        "columns",
        aliases={0: 0, 1: 1},
    )(*[resident(a) for a in (v_ext, w_ext, first, second, packed)])
    first, second = swaps(first, second, "gz")
    v_ext, w_ext = resident(v_ext), resident(w_ext)
    devices = plan.gx * plan.gy * plan.gz
    sums = kept((2 * STEPS + 1, 8, 128))
    sums, rim_v, rim_w, *fields = call(
        functools.partial(inner, plan),
        [sums, rim, rim] + [table] * (4 + STEPS),
        "inner",
        aliases={i: i - 1 for i in range(2, 8 + STEPS)},
        flops=1 << 24,
    )(v_ext, w_ext, *[resident(a) for a in (rim_v, rim_w, *fields)])
    basis = fields[4:]
    rims, moments = call(
        functools.partial(outer, plan),
        [kept((STEPS + 1, plan.rim + 2, plan.tall, 128)), kept((devices, 1, 128))],
        "outer",
        scratch=[rim] * 5,
    )(*[resident(a) for a in (first, second, rim_v, rim_w, sums)])
    parts = lax.all_to_all(moments, AXES, 0, 0, tiled=True)
    chunk = 4
    shape = jax.ShapeDtypeStruct((nx, ny, nz), jnp.float32)
    operands = [parts, v_ext, rims] + basis
    out, residual = pl.pallas_call(
        functools.partial(combine, plan, chunk),
        out_shape=[shape, shape],
        in_specs=[vmem_spec()] * len(operands),
        out_specs=[pl.BlockSpec(memory_space=pl.ANY)] * 2,
        scratch_shapes=[kept((nx, ny, nz))] * 2 + [pltpu.SemaphoreType.DMA((2, nx // chunk))],
        compiler_params=pltpu.CompilerParams(vmem_limit_bytes=40 << 20),
        name="combine",
    )(*[resident(a) for a in operands])
    return out, residual


def solution(mesh):
    placed = P("gx", "gy", "gz")
    return jax.shard_map(
        functools.partial(on_device, mesh),
        mesh=mesh,
        in_specs=(placed,) * 3,
        out_specs=(placed, placed),
        check_vma=False,
    )
```
